256 devices in a mesh: chain: 8 (over z), bond: 32 (over y, x, core).
Axes of the slice: x: 4, y: 4, z: 8, core: 2. Of those that a mesh axis runs over, the one named last changes fastest.
Arguments:
- site_tensors: bfloat16 [8, 1024, 4, 1024], P('chain', 'bond')
- start_env: bfloat16 [4, 1024, 1024], P(None, 'bond'), may hold values from -6 to 6
- operators: float32 [6, 4, 4], replicated, may hold values from -4 to 4
- op_site: int32 [4], replicated, may hold values from 0 to 7
- op_kind: int32 [4], replicated, may hold values from 0 to 5
- probe: float32 [4, 4], replicated
Outputs:
- block_env: bfloat16 [8, 4, 1024, 1024], P('chain', None, 'bond')
- correlation: float32 [4, 8], P(None, 'chain')
The draws below stay inside these ranges and needn't reach their ends.
All inputs are finite; a program needn't handle non-finite values.
Results may differ from the reference program's by a relative error of at most 0.03.
Values may be sent and summed in bfloat16 or wider, within the bound.
No kernel may reach another device: no remote copies, remote signals or barrier semaphores. Data moves between devices by JAX's collectives and lax.ppermute only.
A program may use at most 128 MiB of HBM per device.

```python
import math
import jax
import jax.numpy as jnp
from jax import lax

D = 1024
PHYS = 4
NOPS = 6
FRONTS = 4
SITES = 8


def draw_site_tensors(key, part):
    key = jax.random.fold_in(key, 11)
    base = jax.random.normal(key, (SITES, D, PHYS, D), jnp.float32)
    rowpos = jnp.arange(D, dtype=jnp.float32)
    scaling = jnp.exp(math.log(3.0) * ((rowpos + 0.5) / D - 0.5))
    factor = (2.0 * D * 1.2137) ** (-0.5)
    return (base * scaling[None, :, None, None] * factor).astype(jnp.bfloat16)


def draw_probe(key, part):
    key = jax.random.fold_in(key, 13)
    base = jnp.clip(jax.random.normal(key, (PHYS, PHYS), jnp.float32), -4.0, 4.0)
    level = jnp.trace(base) / PHYS
    return base - level * jnp.eye(PHYS, dtype=jnp.float32)


def with_ends(values, rng, least, high):
    longest = values.shape.index(max(values.shape))
    spots = []
    for shift in (0, 1):
        where = [jax.random.randint(jax.random.fold_in(rng, axis), (), 0, length) for axis, length in enumerate(values.shape)]
        where[longest] = (where[longest] + shift) % values.shape[longest]
        spots.append(tuple(where))
    return values.at[spots[0]].set(least).at[spots[1]].set(high)


def steps_of(key, dims, split, low, largest):
    gain = 1.0
    for position, blocks in split:
        draws = jax.random.uniform(jax.random.fold_in(jax.random.fold_in(key, 6), position), (blocks,), jnp.float32, low / len(split), largest / len(split))
        gain = gain * jnp.repeat(jnp.exp(draws), dims[position] // blocks).reshape((-1,) + (1,) * (len(dims) - 1 - position))
    return gain


def centred(key, extent, scale, most, split=(), held_as=jnp.bfloat16):
    array = scale * jax.random.normal(key, extent, jnp.float32)
    if split:
        array = array * steps_of(key, extent, split, -0.22, 0.18)
    return jnp.clip(array, -most, most).astype(held_as)


def setup_inputs(seed: int = 0) -> dict:
    keys = jax.random.split(jax.random.key(seed), 7)
    site_tensors = draw_site_tensors(jax.random.fold_in(keys[6], 71), 0)
    start_env = centred(keys[1], (FRONTS, D, D), 1.0, 6.0, ((1, 32),))
    operators = centred(keys[2], (NOPS, PHYS, PHYS), 1.0, 4.0, (), jnp.float32)
    op_site = with_ends(jax.random.randint(keys[3], (FRONTS,), 0, SITES), jax.random.fold_in(keys[3], 1), 0, SITES - 1).astype(jnp.int32)
    op_kind = with_ends(jax.random.randint(keys[4], (FRONTS,), 0, NOPS), jax.random.fold_in(keys[4], 1), 0, NOPS - 1).astype(jnp.int32)
    probe = draw_probe(jax.random.fold_in(keys[6], 71), 0)
    return dict(site_tensors=site_tensors, start_env=start_env, operators=operators, op_site=op_site, op_kind=op_kind, probe=probe)


def reference(site_tensors, start_env, operators, op_site, op_kind, probe):
    eye = jnp.eye(PHYS, dtype=jnp.float32)
    onehot = (op_kind[:, None] == jnp.arange(NOPS, dtype=jnp.int32)[None, :]).astype(jnp.float32)
    chosen = jnp.einsum('fn,nst->fst', onehot, operators)

    def one_front(packed):
        carried, place, kind_op = packed
        envs = []
        values = []
        for site in range(SITES):
            tensor = site_tensors[site]
            mixing = jnp.where(place == site, kind_op, eye)
            look = probe
            if site % 2 == 1:
                mixing = mixing.T
                look = probe.T
            prod32 = jnp.dot(carried, tensor.reshape(D, PHYS * D), preferred_element_type=jnp.float32).reshape(D, PHYS, D)
            intersection = jnp.einsum('rsb,rtb->st', tensor.astype(jnp.float32), prod32)
            values.append(jnp.sum(intersection * look) / math.sqrt(D))
            rounded = prod32.astype(jnp.bfloat16)
            mixed = jnp.einsum('st,rtb->rsb', mixing, rounded.astype(jnp.float32)).astype(jnp.bfloat16)
            fresh = lax.dot_general(mixed.reshape(D * PHYS, D), tensor.reshape(D * PHYS, D), (((0,), (0,)), ((), ())), preferred_element_type=jnp.float32)
            carried = fresh.astype(jnp.bfloat16)
            envs.append(carried)
        return (jnp.stack(envs), jnp.stack(values))
    envs, values = lax.map(one_front, (start_env, op_site, chosen))
    return (jnp.transpose(envs, (1, 0, 2, 3)), values)
```

```python
import functools
import math

import jax
import jax.numpy as jnp
from jax import lax
from jax.experimental import pallas as pl
from jax.experimental.pallas import tpu as pltpu
from jax.sharding import PartitionSpec as P

EXTRA = 16
MIB = 1 << 20


def split3(value):
    high = value.astype(jnp.bfloat16)
    rest = value - high.astype(jnp.float32)
    mid = rest.astype(jnp.bfloat16)
    low = (rest - mid.astype(jnp.float32)).astype(jnp.bfloat16)
    return high, mid, low


def first_kernel(turn, group, mix_ref, env_ref, tensor_ref, look_ref, out_ref, total):
    step = pl.program_id(0)
    panel = tensor_ref.shape[2]
    phys = tensor_ref.shape[1]
    width = tensor_ref.shape[0] * panel
    cols = tensor_ref.shape[3]

    @pl.when(step == 0)
    def _():
        total[...] = jnp.zeros_like(total)

    prods = [
        jnp.dot(env_ref[...], tensor_ref[:, t].reshape(width, cols), preferred_element_type=jnp.float32)
        for t in range(phys)
    ]
    for f in range(group):
        rows = slice(f * panel, (f + 1) * panel)
        mine = [prods[t][rows] for t in range(phys)]
        seen = sum(look_ref[t] * mine[t] for t in range(phys))
        line = jnp.sum(seen, axis=0, keepdims=True)
        total[f : f + 1] += sum(line[:, c : c + 128] for c in range(0, cols, 128))
        mixed = [
            sum(mix_ref[turn, f, s, t] * mine[t] for t in range(phys)) for s in range(phys)
        ]
        turned = jnp.concatenate(mixed, axis=0).T.astype(jnp.bfloat16)
        out_ref[pl.ds(step * (cols // panel), cols // panel), rows, :] = turned.reshape(
            cols // panel, panel, phys * panel
        )

    @pl.when(step == pl.num_programs(0) - 1)
    def _():
        value = jnp.broadcast_to(jnp.sum(total[...], axis=1, keepdims=True), total.shape)
        parts = jnp.concatenate([p.astype(jnp.float32) for p in split3(value)], axis=0)
        block = jnp.concatenate([parts, jnp.zeros((EXTRA - parts.shape[0], 128), jnp.float32)], axis=0)
        block = block.astype(jnp.bfloat16)
        out_ref[:, group * panel :, :] = jnp.broadcast_to(block[None], (out_ref.shape[0], EXTRA, 128))


def first(turn, group, mixes, env, tensor, look):
    peers, phys, panel, width = tensor.shape
    cols = 256
    tall = group * panel + EXTRA
    return pl.pallas_call(
        functools.partial(first_kernel, turn, group),
        grid=(width // cols,),
        in_specs=[
            pl.BlockSpec(memory_space=pltpu.SMEM),
            pl.BlockSpec((group * panel, width), lambda i: (0, 0)),
            pl.BlockSpec((peers, phys, panel, cols), lambda i: (0, 0, 0, i)),
            pl.BlockSpec((phys, panel, cols), lambda i: (0, 0, i)),
        ],
        out_specs=pl.BlockSpec((peers, tall, phys * panel), lambda i: (0, 0, 0)),
        out_shape=jax.ShapeDtypeStruct((peers, tall, phys * panel), jnp.bfloat16),
        scratch_shapes=[pltpu.VMEM((group, 128), jnp.float32)],
        compiler_params=pltpu.CompilerParams(vmem_limit_bytes=24 * MIB),
    )(mixes, env, tensor, look)


def second_kernel(rows, moved_ref, tensor_ref, env_ref, sums_ref, acc):
    step = pl.program_id(0)
    chunk = moved_ref.shape[0]
    depth = tensor_ref.shape[1] * tensor_ref.shape[2]

    @pl.when(step == 0)
    def _():
        acc[...] = jnp.zeros_like(acc)
        sums_ref[...] = jnp.zeros_like(sums_ref)

    left = jnp.concatenate([moved_ref[d, :rows] for d in range(chunk)], axis=1)
    right = tensor_ref[...].reshape(chunk * depth, tensor_ref.shape[3])
    acc[...] += jnp.dot(left, right, preferred_element_type=jnp.float32)
    sums_ref[...] += jnp.sum(moved_ref[:, rows:].astype(jnp.float32), axis=0)

    @pl.when(step == pl.num_programs(0) - 1)
    def _():
        env_ref[...] = acc[...].astype(jnp.bfloat16)


def second(group, moved, tensor):
    peers, phys, panel, width = tensor.shape
    chunk = 8
    rows = group * panel
    return pl.pallas_call(
        functools.partial(second_kernel, rows),
        grid=(peers // chunk,),
        in_specs=[
            pl.BlockSpec((chunk,) + moved.shape[1:], lambda i: (i, 0, 0)),
            pl.BlockSpec((chunk, phys, panel, width), lambda i: (i, 0, 0, 0)),
        ],
        out_specs=[
            pl.BlockSpec((rows, width), lambda i: (0, 0)),
            pl.BlockSpec((EXTRA, 128), lambda i: (0, 0)),
        ],
        out_shape=[
            jax.ShapeDtypeStruct((rows, width), jnp.bfloat16),
            jax.ShapeDtypeStruct((EXTRA, 128), jnp.float32),
        ],
        scratch_shapes=[pltpu.VMEM((rows, width), jnp.float32)],
        compiler_params=pltpu.CompilerParams(vmem_limit_bytes=24 * MIB),
    )(moved, tensor)


def on_device(site_tensors, start_env, operators, op_site, op_kind, probe):
    fronts, panel, width = start_env.shape
    phys = site_tensors.shape[2]
    kinds = operators.shape[0]
    links = lax.axis_size("chain")
    link = lax.axis_index("chain")
    group = 2
    groups = fronts // group
    turns = links + groups - 1
    mine = jnp.swapaxes(site_tensors[0], 0, 1)
    tensor = lax.all_gather(mine, "bond", axis=0)
    is_odd = link % 2 == 1
    eye = jnp.eye(phys, dtype=jnp.float32)
    onehot = (op_kind[:, None] == jnp.arange(kinds, dtype=jnp.int32)[None, :]).astype(jnp.float32)
    chosen = jnp.sum(onehot[:, :, None, None] * operators[None], axis=1)
    mixes = jnp.where((op_site == link)[:, None, None], chosen, eye[None])
    mixes = jnp.where(is_odd, jnp.swapaxes(mixes, 1, 2), mixes)
    slots = jnp.clip(jnp.arange(turns) - link, 0, groups - 1)
    mixes = mixes.reshape(groups, group, phys, phys)
    per_turn = jnp.where((slots == 0)[:, None, None, None], mixes[0][None], mixes[1][None])
    looking = jnp.where(is_odd, probe.T, probe) / math.sqrt(width)
    mine32 = mine.astype(jnp.float32)
    look = jnp.stack([sum(looking[s, t] * mine32[s] for s in range(phys)) for t in range(phys)])
    starts = start_env.reshape(groups, group * panel, width)
    env = starts[0]
    envs, sums = [], []
    for turn in range(turns):
        if 0 < turn < groups:
            env = jnp.where(link == 0, starts[turn], env)
        sent = first(turn, group, per_turn, env, tensor, look)
        moved = lax.all_to_all(sent, "bond", 0, 0, tiled=True)
        fresh, total = second(group, moved, tensor)
        envs.append(fresh)
        sums.append(total)
        if turn + 1 < turns:
            env = lax.ppermute(fresh, "chain", [(i, i + 1) for i in range(links - 1)])
    picked = lax.dynamic_slice_in_dim(jnp.stack(envs), link, groups, 0)
    values = lax.dynamic_slice_in_dim(jnp.stack(sums), link, groups, 0)[:, :, 0]
    values = values[:, : 3 * group].reshape(groups, 3, group).sum(axis=1)
    return picked.reshape(1, fronts, panel, width), values.reshape(fronts, 1)


def solution(mesh):
    placed = (P("chain", "bond", None, None), P(None, "bond", None), P(), P(), P(), P())
    return jax.shard_map(
        on_device,
        mesh=mesh,
        in_specs=placed,
        out_specs=(P("chain", None, "bond", None), P(None, "chain")),
        check_vma=False,
    )
```

```python
import functools
import math

import jax
import jax.numpy as jnp
from jax import lax
from jax.experimental import pallas as pl
from jax.experimental.pallas import tpu as pltpu
from jax.sharding import Mesh
from jax.sharding import PartitionSpec as P

EXTRA = 16
MIB = 1 << 20
COLS = 256


def split3(value):
    high = value.astype(jnp.bfloat16).astype(jnp.float32)
    rest = value - high
    mid = rest.astype(jnp.bfloat16).astype(jnp.float32)
    return high, mid, rest - mid


def parts_of(value, lanes):
    rows = [jnp.broadcast_to(p, (1, lanes)) for p in split3(value)]
    rows.append(jnp.zeros((EXTRA - 3, lanes), jnp.float32))
    return jnp.concatenate(rows, axis=0).astype(jnp.bfloat16)


def spread(turn, where_ref, mix_ref, look_ref, env, tensor_ref, out_ref):
    peers, phys, panel, width = tensor_ref.shape
    mem = where_ref[0]
    half = peers // 2
    total = jnp.zeros((1, 128), jnp.float32)
    for c in range(width // COLS):
        cols = slice(c * COLS, (c + 1) * COLS)
        prods = [
            jnp.dot(
                env,
                tensor_ref[:, t, :, cols].reshape(width, COLS),
                preferred_element_type=jnp.float32,
            )
            for t in range(phys)
        ]
        for s in range(phys):
            own = jnp.concatenate(
                [tensor_ref[h * half + mem, s, :, cols] for h in range(2)], axis=0
            ).astype(jnp.float32)
            seen = own * sum(look_ref[turn % 2, s, t] * prods[t] for t in range(phys))
            line = jnp.sum(seen, axis=0, keepdims=True)
            total += sum(line[:, b : b + 128] for b in range(0, COLS, 128))
        mixed = [sum(mix_ref[turn % 2, s, t] * prods[t] for t in range(phys)) for s in range(phys)]
        tall = jnp.concatenate(
            [mixed[s][h * panel : (h + 1) * panel] for h in range(2) for s in range(phys)], axis=0
        )
        turned = tall.astype(jnp.bfloat16).T.reshape(COLS // panel, panel, 2 * phys * panel)
        block = c * (COLS // panel)
        h = block // half
        block = block % half
        out_ref[block : block + COLS // panel, h * panel : (h + 1) * panel, :] = turned
    return jnp.sum(total, axis=1, keepdims=True)


def gather(moved_ref, tensor_ref, env_ref):
    peers, phys, panel, width = tensor_ref.shape
    half = peers // 2
    rows = 2 * panel
    left = jnp.concatenate([moved_ref[g, :rows] for g in range(half)], axis=1)
    for c in range(width // COLS):
        cols = slice(c * COLS, (c + 1) * COLS)
        right = jnp.concatenate(
            [
                tensor_ref[h * half + g, :, :, cols].reshape(phys * panel, COLS)
                for g in range(half)
                for h in range(2)
            ],
            axis=0,
        )
        env_ref[:, cols] = jnp.dot(left, right, preferred_element_type=jnp.float32).astype(jnp.bfloat16)


def first_kernel(turn, where_ref, mix_ref, look_ref, env_ref, tensor_ref, seen_ref, out_ref, new_ref):
    value = spread(turn, where_ref, mix_ref, look_ref, env_ref[...], tensor_ref, out_ref)
    new_ref[0] = jnp.where(where_ref[1] == turn // 2, value, seen_ref[0])
    new_ref[1] = seen_ref[1]


def middle_kernel(
    turn, last, where_ref, mix_ref, look_ref, moved_ref, even_ref, odd_ref, kept_ref, seen_ref,
    out_ref, keep_ref, new_ref, env_ref,
):
    now = where_ref[1] == turn // 2
    gather(moved_ref, even_ref, env_ref)
    keep_ref[...] = jnp.where(now, env_ref[...], kept_ref[...])
    value = spread(turn, where_ref, mix_ref, look_ref, env_ref[...], odd_ref, out_ref)
    value = jnp.where(now, value, seen_ref[1])
    new_ref[0] = seen_ref[0]
    new_ref[1] = value
    if last:
        rows, lanes = env_ref.shape[0], out_ref.shape[2]
        block = jnp.concatenate(
            [parts_of(v[:1, :1], lanes // 2) for v in (seen_ref[0], value)], axis=1
        )
        out_ref[:, rows:, :] = jnp.broadcast_to(block[None], (out_ref.shape[0], EXTRA, lanes))


def second_kernel(turn, where_ref, moved_ref, tensor_ref, kept_ref, env_ref, keep_ref):
    gather(moved_ref, tensor_ref, env_ref)
    keep_ref[...] = jnp.where(where_ref[1] == turn // 2, env_ref[...], kept_ref[...])


def home_kernel(turn, where_ref, moved_ref, tensor_ref, even_ref, odd_ref, out_ref, env):
    gather(moved_ref, tensor_ref, env)
    panel = tensor_ref.shape[2]
    rows = 2 * panel
    now = where_ref[1] == turn // 2
    values = jnp.sum(moved_ref[:, rows:].astype(jnp.float32), axis=0)
    for q in range(2):
        block = even_ref[...] if q == 0 else jnp.where(now, env[...], odd_ref[...])
        value = jnp.sum(values[:, q * 128 : q * 128 + 1], axis=0, keepdims=True)
        extra = parts_of(value, out_ref.shape[2])
        for h in range(2):
            out_ref[2 * q + h, :panel] = block[h * panel : (h + 1) * panel]
            out_ref[2 * q + h, panel:] = extra


def lay_kernel(side, where_ref, *refs):
    pieces, out_ref, sems = refs[:-2], refs[-2], refs[-1]
    y, x, core = where_ref[2], where_ref[3], where_ref[4]
    wide = out_ref.shape[3] // 2
    copies = []
    count = len(pieces) // 2
    for source in range(2):
        at = core if source == 0 else 1 - core
        for p in range(count):
            ref = pieces[source * count + p]
            for j in range(ref.shape[0]):
                if p == 0:
                    m, k = 0, j
                elif p < side:
                    m, k = p, 0
                else:
                    m, k = p - side + 1, j + 1
                along = lax.rem(y + side - jnp.where(at == 0, m, k), side)
                across = lax.rem(x + side - jnp.where(at == 0, k, m), side)
                chip = along * side + across
                copies.append(
                    pltpu.make_async_copy(
                        ref.at[j],
                        out_ref.at[pl.ds(2 * chip, 2), :, :, pl.ds(pl.multiple_of(at * wide, wide), wide)],
                        sems.at[len(copies)],
                    )
                )
    for copy in copies:
        copy.start()
    for copy in copies:
        copy.wait()


SMEM = pl.BlockSpec(memory_space=pltpu.SMEM)
VMEM = pl.BlockSpec(memory_space=pltpu.VMEM)


def params():
    return pltpu.CompilerParams(vmem_limit_bytes=24 * MIB)


def shifts(side, by, first):
    pairs = []
    for y in range(side):
        for x in range(side):
            for core in range(2):
                across = (core == 0) == first
                to = y * side + (x + by) % side if across else (y + by) % side * side + x
                pairs.append(((y * side + x) * 2 + core, to * 2 + core))
    return pairs


def gathered(where, own, core, side):
    bond = ("half", "member")
    swap = [(i, i ^ 1) for i in range(2 * side * side)]
    phys, panel, width = own.shape
    low, high = own[..., : width // 2], own[..., width // 2 :]
    other = lax.ppermute(jnp.where(core == 0, high, low), bond, swap)
    keep = jnp.where(core == 0, low, high)
    chip = jnp.where(core == 0, jnp.stack([keep, other]), jnp.stack([other, keep]))
    near = [lax.ppermute(chip, bond, shifts(side, k, True)) for k in range(1, side)]
    far = [lax.ppermute(chip, bond, shifts(side, m, False)) for m in range(1, side)]
    bundle = jnp.stack(near)
    pieces = [jnp.stack([chip] + near)] + [f[None] for f in far]
    pieces += [lax.ppermute(bundle, bond, shifts(side, m, False)) for m in range(1, side)]
    swapped = [lax.ppermute(p, bond, swap) for p in pieces]
    peers = 2 * side * side
    return pl.pallas_call(
        functools.partial(lay_kernel, side),
        in_specs=[SMEM] + [pl.BlockSpec(memory_space=pl.ANY)] * (2 * len(pieces)),
        out_specs=pl.BlockSpec(memory_space=pl.ANY),
        out_shape=jax.ShapeDtypeStruct((peers, phys, panel, width), jnp.bfloat16),
        scratch_shapes=[pltpu.SemaphoreType.DMA((2 * side * side,))],
        compiler_params=params(),
    )(where, *pieces, *swapped)


def on_device(site_tensors, start_env, operators, op_site, op_kind, probe):
    fronts, panel, width = start_env.shape
    phys = site_tensors.shape[2]
    kinds = operators.shape[0]
    pairs = lax.axis_size("pair")
    pair = lax.axis_index("pair")
    parity = lax.axis_index("parity")
    half = lax.axis_index("half")
    member = lax.axis_index("member")
    members = lax.axis_size("member")
    side = math.isqrt(members)
    turns = 2 * pairs
    rows = 2 * panel
    lanes = 2 * phys * panel
    f32 = jnp.float32
    core = member % 2
    chip = half * (members // 2) + member // 2
    where = jnp.stack([member, pair, chip // side, chip % side, core]).astype(jnp.int32)

    mine = jnp.swapaxes(site_tensors[0], 0, 1)
    near = lax.ppermute(mine, "parity", [(0, 1), (1, 0)])
    later = lax.all_gather(jnp.where(parity == 0, near, mine), ("half", "member"), axis=0)
    tensors = [gathered(where, jnp.where(parity == 0, mine, near), core, side), later]
    tensors = [pltpu.with_memory_space_constraint(t, pltpu.VMEM) for t in tensors]

    front = 2 * parity + half
    kind = lax.dynamic_index_in_dim(op_kind, front, 0, keepdims=False)
    site = lax.dynamic_index_in_dim(op_site, front, 0, keepdims=False)
    onehot = (kind == jnp.arange(kinds, dtype=jnp.int32)).astype(f32)
    chosen = jnp.sum(onehot[:, None, None] * operators, axis=0)
    eye = jnp.eye(phys, dtype=f32)
    even = jnp.where(site == 2 * pair, chosen, eye)
    odd = jnp.where(site == 2 * pair + 1, chosen, eye)
    mixes = jnp.stack([even, odd.T])
    looks = jnp.stack([probe, probe.T]) / math.sqrt(width)

    given = lax.dynamic_index_in_dim(start_env, 2 * parity + 1 - half, 0, keepdims=False)
    other = lax.ppermute(given, "half", [(0, 1), (1, 0)])
    own = lax.dynamic_index_in_dim(start_env, front, 0, keepdims=False)
    env = jnp.where(half == 0, jnp.concatenate([own, other]), jnp.concatenate([other, own]))

    seen_shape = jax.ShapeDtypeStruct((2, 8, 128), f32)
    env_shape = jax.ShapeDtypeStruct((rows, width), jnp.bfloat16)
    kept = [env, env]
    seen = jnp.zeros(seen_shape.shape, f32)
    moved = None
    for turn in range(turns):
        slot = turn % 2
        last = turn == turns - 1
        out_shape = jax.ShapeDtypeStruct((members, rows + (EXTRA if last else 0), lanes), jnp.bfloat16)
        if slot == 0:
            sent, seen = pl.pallas_call(
                functools.partial(first_kernel, turn),
                in_specs=[SMEM, SMEM, SMEM, VMEM, VMEM, VMEM],
                out_specs=[VMEM, VMEM],
                out_shape=[out_shape, seen_shape],
                compiler_params=params(),
            )(where, mixes, looks, env, tensors[0], seen)
        else:
            sent, kept[0], seen = pl.pallas_call(
                functools.partial(middle_kernel, turn, last),
                in_specs=[SMEM, SMEM, SMEM, VMEM, VMEM, VMEM, VMEM, VMEM],
                out_specs=[VMEM, VMEM, VMEM],
                out_shape=[out_shape, env_shape, seen_shape],
                scratch_shapes=[pltpu.VMEM((rows, width), jnp.bfloat16)],
                compiler_params=params(),
            )(where, mixes, looks, moved, *tensors, kept[0], seen)
        moved = lax.all_to_all(sent, "member", 0, 0, tiled=True)
        if slot == 1 and not last:
            fresh, kept[1] = pl.pallas_call(
                functools.partial(second_kernel, turn),
                in_specs=[SMEM, VMEM, VMEM, VMEM],
                out_specs=[VMEM, VMEM],
                out_shape=[env_shape, env_shape],
                compiler_params=params(),
            )(where, moved, tensors[1], kept[1])
            env = lax.ppermute(fresh, "pair", [(i, i + 1) for i in range(pairs - 1)])
    homeward = pl.pallas_call(
        functools.partial(home_kernel, turns - 1),
        in_specs=[SMEM, VMEM, VMEM, VMEM, VMEM],
        out_specs=VMEM,
        out_shape=jax.ShapeDtypeStruct((fronts, panel + EXTRA, width), jnp.bfloat16),
        scratch_shapes=[pltpu.VMEM((rows, width), jnp.bfloat16)],
        compiler_params=params(),
    )(where, moved, tensors[1], kept[0], kept[1])
    home = lax.all_to_all(homeward, ("parity", "half"), 0, 0, tiled=True)
    values = jnp.sum(home[:, panel : panel + 3, 0].astype(f32), axis=1)
    return home[None, :, :panel], values[:, None]


def solution(mesh):
    links, peers = mesh.devices.shape
    devices = mesh.devices.reshape(links // 2, 2, 2, peers // 2)
    chain, bond = ("pair", "parity"), ("half", "member")
    placed = (P(chain, bond, None, None), P(None, bond, None), P(), P(), P(), P())
    return jax.shard_map(
        on_device,
        mesh=Mesh(devices, chain + bond),
        in_specs=placed,
        out_specs=(P(chain, None, bond, None), P(None, chain)),
        check_vma=False,
    )
```

```python
import functools
import math

import jax
import jax.numpy as jnp
from jax import lax
from jax.experimental import pallas as pl
from jax.experimental.pallas import tpu as pltpu
from jax.sharding import Mesh
from jax.sharding import PartitionSpec as P

EXTRA = 16
MIB = 1 << 20
COLS = 256


def split3(value):
    high = value.astype(jnp.bfloat16).astype(jnp.float32)
    rest = value - high
    mid = rest.astype(jnp.bfloat16).astype(jnp.float32)
    return high, mid, rest - mid


def parts_of(value, lanes):
    rows = [jnp.broadcast_to(p, (1, lanes)) for p in split3(value)]
    rows.append(jnp.zeros((EXTRA - 3, lanes), jnp.float32))
    return jnp.concatenate(rows, axis=0).astype(jnp.bfloat16)


def columns(tensor_ref, t, c):
    if len(tensor_ref.shape) == 4:
        return tensor_ref[:, t, :, c * COLS : (c + 1) * COLS].reshape(-1, COLS)
    per = tensor_ref.shape[5] // COLS
    at = c % per * COLS
    return tensor_ref[:, c // per, :, t, :, at : at + COLS].reshape(-1, COLS)


def block(tensor_ref, d, s, c):
    if len(tensor_ref.shape) == 4:
        return tensor_ref[d, s, :, c * COLS : (c + 1) * COLS].reshape(-1, COLS)
    per = tensor_ref.shape[5] // COLS
    at = c % per * COLS
    return tensor_ref[d // 2, c // per, d % 2, s, :, at : at + COLS].reshape(-1, COLS)


def spread(slot, where_ref, mix_ref, look_ref, env, tensor_ref, out_ref, arrived=None):
    width = env.shape[1]
    phys = mix_ref.shape[1]
    panel = env.shape[0] // 2
    half = width // panel // 2
    mem = where_ref[0]
    total = jnp.zeros((1, 128), jnp.float32)
    for c in range(width // COLS):
        if arrived is not None:
            arrived[c]()
        prods = [
            jnp.dot(env, columns(tensor_ref, t, c), preferred_element_type=jnp.float32)
            for t in range(phys)
        ]
        for s in range(phys):
            own = jnp.concatenate(
                [block(tensor_ref, h * half + mem, s, c) for h in range(2)], axis=0
            ).astype(jnp.float32)
            seen = own * sum(look_ref[slot, s, t] * prods[t] for t in range(phys))
            line = jnp.sum(seen, axis=0, keepdims=True)
            total += sum(line[:, b : b + 128] for b in range(0, COLS, 128))
        mixed = [sum(mix_ref[slot, s, t] * prods[t] for t in range(phys)) for s in range(phys)]
        tall = jnp.concatenate(
            [mixed[s][h * panel : (h + 1) * panel] for h in range(2) for s in range(phys)], axis=0
        )
        turned = tall.astype(jnp.bfloat16).T.reshape(COLS // panel, panel, 2 * phys * panel)
        first = c * (COLS // panel)
        h, first = first // half, first % half
        out_ref[first : first + COLS // panel, h * panel : (h + 1) * panel, :] = turned
    return jnp.sum(total, axis=1, keepdims=True)


def gather(moved_ref, tensor_ref, env_ref):
    rows, width = env_ref.shape
    half = moved_ref.shape[0]
    if moved_ref.shape[1] < rows:
        left = [
            jnp.concatenate([moved_ref[g], moved_ref[g + 1]], axis=0) for g in range(0, half, 2)
        ]
    else:
        left = [moved_ref[g, :rows] for g in range(half)]
    left = jnp.concatenate(left, axis=1)
    for c in range(width // COLS):
        right = jnp.concatenate(
            [
                block(tensor_ref, h * half + g, slice(None), c)
                for g in range(half)
                for h in range(2)
            ],
            axis=0,
        )
        env_ref[:, c * COLS : (c + 1) * COLS] = jnp.dot(
            left, right, preferred_element_type=jnp.float32
        ).astype(jnp.bfloat16)


def chip_of(side, where_ref, at, m, k):
    y, x = where_ref[2], where_ref[3]
    along = lax.rem(y + side - jnp.where(at == 0, m, k), side)
    across = lax.rem(x + side - jnp.where(at == 0, k, m), side)
    return along * side + across


def lay(side, where_ref, pieces, tensor_ref, sems):
    copies = []
    for i, ref in enumerate(pieces):
        at = where_ref[4] if i < side else 1 - where_ref[4]
        for k in range(side):
            place = tensor_ref.at[chip_of(side, where_ref, at, i % side, k), at]
            copies.append(pltpu.make_async_copy(ref.at[k], place, sems.at[i, k]))
    for copy in copies:
        copy.start()
    for copy in copies:
        copy.wait()


def lay_kernel(side, where_ref, *refs):
    lay(side, where_ref, refs[:-2], refs[-2], refs[-1])


def pieces_kernel(side, where_ref, moved_ref, *refs):
    pieces, (env_ref, tensor, sems) = refs[:-3], refs[-3:]
    lay(side, where_ref, pieces, tensor, sems)
    gather(moved_ref, tensor, env_ref)


def stream_kernel(
    now, where_ref, mix_ref, look_ref, env_ref, tensor_ref, seen_ref, out_ref, new_ref, held, sems
):
    copies = []
    for c in range(held.shape[3] // COLS):
        cols = pl.ds(c * COLS, COLS)
        copies.append(
            pltpu.make_async_copy(
                tensor_ref.at[:, :, :, cols], held.at[:, :, :, cols], sems.at[c]
            )
        )
        copies[-1].start()
    arrived = [copy.wait for copy in copies]
    value = spread(1, where_ref, mix_ref, look_ref, env_ref[...], held, out_ref, arrived)
    new_ref[0] = seen_ref[0]
    new_ref[1] = jnp.broadcast_to(value, new_ref.shape[1:])


def start_kernel(side, where_ref, mix_ref, look_ref, env_ref, twin_ref, *refs):
    pieces, (out_ref, new_ref, tensor, sems) = refs[:-4], refs[-4:]
    core = where_ref[4]
    copies = []
    for m, ref in enumerate(pieces):
        for k in range(side):
            place = tensor.at[chip_of(side, where_ref, core, m, k)]
            copies.append(pltpu.make_async_copy(ref.at[k], place, sems.at[m, k]))
    for copy in copies:
        copy.start()
    own, twin = env_ref[...], twin_ref[...]
    env = jnp.concatenate(
        [jnp.where(core == 0, own, twin), jnp.where(core == 0, twin, own)], axis=0
    )
    for copy in copies:
        copy.wait()
    chips, _, phys, panel, wide = tensor.shape
    mem = where_ref[0] // 2
    total = jnp.zeros((1, 128), jnp.float32)
    for c in range(wide // COLS):
        cols = slice(c * COLS, (c + 1) * COLS)
        prods = [
            jnp.dot(
                env, tensor[:, :, t, :, cols].reshape(-1, COLS), preferred_element_type=jnp.float32
            )
            for t in range(phys)
        ]
        for s in range(phys):
            rows = [tensor[h * (chips // 2) + mem, o, s, :, cols] for o in range(2) for h in range(2)]
            seen = jnp.concatenate(rows, axis=0).astype(jnp.float32)
            seen = seen * sum(look_ref[0, s, t] * prods[t] for t in range(phys))
            line = jnp.sum(seen, axis=0, keepdims=True)
            total += sum(line[:, b : b + 128] for b in range(0, COLS, 128))
        mixed = [sum(mix_ref[0, s, t] * prods[t] for t in range(phys)) for s in range(phys)]
        tall = [mixed[s][q * panel : (q + 1) * panel] for q in range(4) for s in range(phys)]
        turned = jnp.concatenate(tall, axis=0).astype(jnp.bfloat16).T
        per = COLS // panel
        out_ref[c * per : (c + 1) * per] = turned.reshape(per, panel, 4 * phys * panel)
    value = jnp.sum(total, axis=1, keepdims=True)
    new_ref[...] = jnp.broadcast_to(value, new_ref.shape)


def first_kernel(now, where_ref, mix_ref, look_ref, env_ref, tensor_ref, seen_ref, out_ref, new_ref):
    value = spread(0, where_ref, mix_ref, look_ref, env_ref[...], tensor_ref, out_ref)
    new_ref[0] = jnp.where(where_ref[1] == now, value, seen_ref[0])
    new_ref[1] = seen_ref[1]


def middle_kernel(
    now, where_ref, mix_ref, look_ref, moved_ref, old_ref, tensor_ref, seen_ref, out_ref, new_ref, env_ref
):
    gather(moved_ref, old_ref, env_ref)
    value = spread(1, where_ref, mix_ref, look_ref, env_ref[...], tensor_ref, out_ref)
    new_ref[0] = seen_ref[0]
    new_ref[1] = jnp.where(where_ref[1] == now, value, seen_ref[1])


def end_kernel(
    now, where_ref, mix_ref, look_ref, moved_ref, old_ref, tensor_ref, seen_ref, out_ref, env_ref
):
    gather(moved_ref, old_ref, env_ref)
    value = spread(1, where_ref, mix_ref, look_ref, env_ref[...], tensor_ref, out_ref)
    rows, lanes = env_ref.shape[0], out_ref.shape[2]
    odd = jnp.where(where_ref[1] == now, value, seen_ref[1][:1, :1])
    extra = jnp.concatenate([parts_of(v, lanes // 2) for v in (seen_ref[0][:1, :1], odd)], axis=1)
    out_ref[:, rows:, :] = jnp.broadcast_to(extra[None], (out_ref.shape[0], EXTRA, lanes))


def second_kernel(moved_ref, tensor_ref, env_ref):
    gather(moved_ref, tensor_ref, env_ref)


def home_kernel(where_ref, moved_ref, tensor_ref, *refs):
    kept, (out_ref, env, picked, sems) = refs[:-4], refs[-4:]
    count = (len(kept) + 1) // 2
    rows = env.shape[0]
    panel = rows // 2

    def each(act):
        for i, ref in enumerate(kept):
            q, p = i // count, i % count
            copy = pltpu.make_async_copy(ref, picked.at[q], sems.at[q])
            pl.when(where_ref[1] == p)(getattr(copy, act))

    each("start")
    gather(moved_ref, tensor_ref, env)
    each("wait")
    now = where_ref[1] == count - 1
    values = jnp.sum(moved_ref[:, rows:].astype(jnp.float32), axis=0)
    for q in range(2):
        result = picked[0] if q == 0 else jnp.where(now, env[...], picked[1])
        value = jnp.sum(values[:, q * 128 : q * 128 + 1], axis=0, keepdims=True)
        extra = parts_of(value, out_ref.shape[2])
        for h in range(2):
            out_ref[2 * q + h, :panel] = result[h * panel : (h + 1) * panel]
            out_ref[2 * q + h, panel:] = extra


def mix_kernel(width, where_ref, site_ref, kind_ref, operators_ref, probe_ref, mix_ref, look_ref):
    pair, front = where_ref[1], where_ref[6]
    kind, site = kind_ref[front], site_ref[front]
    phys = probe_ref.shape[0]
    scale = 1.0 / math.sqrt(width)
    for slot in range(2):
        for s in range(phys):
            for t in range(phys):
                row, col = (s, t) if slot == 0 else (t, s)
                own = 1.0 if s == t else 0.0
                mix_ref[slot, s, t] = jnp.where(
                    site == 2 * pair + slot, operators_ref[kind, row, col], own
                )
                look_ref[slot, s, t] = probe_ref[row, col] * scale


def cut_kernel(
    where_ref, mine_ref, near_ref, start_ref, other_ref, later_ref, keep_ref, give_ref, env_ref, sem
):
    core, half, front, parity = where_ref[4], where_ref[5], where_ref[6], where_ref[7]
    panel = other_ref.shape[0]
    copy = pltpu.make_async_copy(
        start_ref.at[front], env_ref.at[pl.ds(pl.multiple_of(half * panel, panel), panel)], sem.at[0]
    )
    copy.start()
    env_ref[pl.ds(pl.multiple_of((1 - half) * panel, panel), panel)] = other_ref[...]
    wide = keep_ref.shape[2]
    mine, near = mine_ref[...], near_ref[...]
    later_ref[...] = jnp.where(parity == 0, near, mine)
    begun = jnp.where(parity == 0, mine, near)
    low, high = begun[..., :wide], begun[..., wide:]
    keep_ref[...] = jnp.where(core == 0, low, high)
    give_ref[...] = jnp.where(core == 0, high, low)
    copy.wait()


SMEM = pl.BlockSpec(memory_space=pltpu.SMEM)
VMEM = pl.BlockSpec(memory_space=pltpu.VMEM)
ANY = pl.BlockSpec(memory_space=pl.ANY)
HBM = pl.BlockSpec(memory_space=pltpu.HBM)


def params():
    return pltpu.CompilerParams(vmem_limit_bytes=16 * MIB)


def shifts(side, by, first):
    pairs = []
    for y in range(side):
        for x in range(side):
            for core in range(2):
                across = (core == 0) == first
                to = y * side + (x + by) % side if across else (y + by) % side * side + x
                pairs.append(((y * side + x) * 2 + core, to * 2 + core))
    return pairs


def in_hbm(arrays):
    return [pltpu.with_memory_space_constraint(a, pltpu.HBM) for a in arrays]


def first_ring(keep, give, core, side):
    bond = ("half", "member")
    other = lax.ppermute(give, bond, twins(side))
    chip = jnp.where(core == 0, jnp.stack([keep, other]), jnp.stack([other, keep]))
    return jnp.stack([chip] + [lax.ppermute(chip, bond, shifts(side, k, True)) for k in range(1, side)])


def second_ring(row, side):
    bond = ("half", "member")
    return [row] + [lax.ppermute(row, bond, shifts(side, m, False)) for m in range(1, side)]


def swap_cores(pieces, side):
    return [lax.ppermute(p, ("half", "member"), twins(side)) for p in pieces]


def twins(side):
    return [(i, i ^ 1) for i in range(2 * side * side)]


def on_device(site_tensors, start_env, operators, op_site, op_kind, probe):
    fronts, panel, width = start_env.shape
    phys = site_tensors.shape[2]
    kinds = operators.shape[0]
    pairs = lax.axis_size("pair")
    pair = lax.axis_index("pair")
    parity = lax.axis_index("parity")
    half = lax.axis_index("half")
    member = lax.axis_index("member")
    members = lax.axis_size("member")
    side = math.isqrt(members)
    rows = 2 * panel
    lanes = 2 * phys * panel
    f32 = jnp.float32
    bf16 = jnp.bfloat16
    core = member % 2
    chip = half * (members // 2) + member // 2
    front = 2 * parity + half
    where = jnp.stack([member, pair, chip // side, chip % side, core, half, front, parity]).astype(jnp.int32)

    mine = jnp.swapaxes(site_tensors[0], 0, 1)
    near = lax.ppermute(mine, "parity", [(0, 1), (1, 0)])
    given = lax.dynamic_index_in_dim(start_env, 2 * parity + 1 - half, 0, keepdims=False)
    other = lax.ppermute(given, "half", [(0, 1), (1, 0)])
    env_shape = jax.ShapeDtypeStruct((rows, width), bf16)
    square = jax.ShapeDtypeStruct((2, phys, phys), f32)
    part = jax.ShapeDtypeStruct((phys, panel, width // 2), bf16)
    bond = ("half", "member")
    mixes, looks = pl.pallas_call(
        functools.partial(mix_kernel, width),
        in_specs=[SMEM] * 5,
        out_specs=[SMEM] * 2,
        out_shape=[square, square],
        compiler_params=params(),
    )(where, op_site, op_kind, operators, probe)
    where, other, mine, near, mixes, looks = lax.optimization_barrier(
        (where, other, mine, near, mixes, looks)
    )
    small = (where, mixes, looks)
    later, keep, give, env = pl.pallas_call(
        cut_kernel,
        in_specs=[SMEM] + [VMEM] * 2 + [ANY, VMEM],
        out_specs=[VMEM] * 4,
        out_shape=[jax.ShapeDtypeStruct(mine.shape, bf16), part, part, env_shape],
        scratch_shapes=[pltpu.SemaphoreType.DMA((1,))],
        compiler_params=params(),
    )(where, mine, near, start_env, other)
    after = lax.all_gather(later, bond, axis=0)
    twin = lax.ppermute(env, bond, twins(side))
    row = first_ring(keep, give, core, side)
    row, twin = lax.optimization_barrier((row, twin))
    pieces = second_ring(row, side)
    swapped = swap_cores(pieces, side)

    def sent_shape(extra):
        return jax.ShapeDtypeStruct((members, rows + extra, lanes), bf16)

    seen_shape = jax.ShapeDtypeStruct((2, 8, 128), f32)

    def exchange(sent):
        return lax.all_to_all(sent, "member", 0, 0, tiled=True)

    sent, seen = pl.pallas_call(
        functools.partial(start_kernel, side),
        in_specs=[SMEM] * 3 + [VMEM] * 2 + [HBM] * side,
        out_specs=[VMEM] * 2,
        out_shape=[jax.ShapeDtypeStruct((members, panel, 2 * lanes), bf16), seen_shape],
        scratch_shapes=[
            pltpu.VMEM((side * side, 2, phys, panel, width // 2), bf16),
            pltpu.SemaphoreType.DMA((side, side)),
        ],
        compiler_params=params(),
    )(*small, env, twin, *in_hbm(pieces))
    moved = exchange(sent)
    whole = (side * side, 2, 2, phys, panel, width // 2)
    lay_sems = pltpu.SemaphoreType.DMA((2 * side, side))
    everything = pieces + swapped
    env = pl.pallas_call(
        functools.partial(pieces_kernel, side),
        in_specs=[SMEM, VMEM] + [HBM] * (2 * side),
        out_specs=VMEM,
        out_shape=env_shape,
        scratch_shapes=[pltpu.VMEM(whole, bf16), lay_sems],
        compiler_params=params(),
    )(where, moved, *in_hbm(everything))
    evens, odds = [env], []
    env, after = lax.optimization_barrier((env, after))
    sent, seen = pl.pallas_call(
        functools.partial(stream_kernel, 0),
        in_specs=[SMEM] * 3 + [VMEM, HBM, VMEM],
        out_specs=[VMEM] * 2,
        out_shape=[sent_shape(0), seen_shape],
        scratch_shapes=[
            pltpu.VMEM(after.shape, bf16),
            pltpu.SemaphoreType.DMA((width // COLS,)),
        ],
        compiler_params=params(),
    )(*small, env, *in_hbm([after]), seen)
    after = pltpu.with_memory_space_constraint(after, pltpu.VMEM)
    before = None
    for now in range(pairs - 1):
        if now > 0:
            sent, seen, env = pl.pallas_call(
                functools.partial(middle_kernel, now),
                in_specs=[SMEM] * 3 + [VMEM] * 4,
                out_specs=[VMEM] * 3,
                out_shape=[sent_shape(0), seen_shape, env_shape],
                compiler_params=params(),
            )(*small, exchange(sent), before, after, seen)
            evens.append(env)
        env = pl.pallas_call(
            second_kernel,
            in_specs=[VMEM] * 2,
            out_specs=VMEM,
            out_shape=env_shape,
            compiler_params=params(),
        )(exchange(sent), after)
        odds.append(env)
        if now == 0:
            env, everything = lax.optimization_barrier((env, everything))
            before = pl.pallas_call(
                functools.partial(lay_kernel, side),
                in_specs=[SMEM] + [HBM] * (2 * side),
                out_specs=ANY,
                out_shape=jax.ShapeDtypeStruct(whole, bf16),
                scratch_shapes=[lay_sems],
                compiler_params=params(),
            )(where, *in_hbm(everything))
            before = pltpu.with_memory_space_constraint(before, pltpu.VMEM)
        env = lax.ppermute(env, "pair", [(now, now + 1)])
        sent, seen = pl.pallas_call(
            functools.partial(first_kernel, now + 1),
            in_specs=[SMEM] * 3 + [VMEM] * 3,
            out_specs=[VMEM] * 2,
            out_shape=[sent_shape(0), seen_shape],
            compiler_params=params(),
        )(*small, env, before, seen)
    moved = exchange(sent)
    sent, env = pl.pallas_call(
        functools.partial(end_kernel, pairs - 1),
        in_specs=[SMEM] * 3 + [VMEM] * 4,
        out_specs=[VMEM] * 2,
        out_shape=[sent_shape(EXTRA), env_shape],
        compiler_params=params(),
    )(*small, moved, before, after, seen)
    evens.append(env)
    kept = evens + odds
    homeward = pl.pallas_call(
        home_kernel,
        in_specs=[SMEM] + [VMEM] * 2 + [ANY] * len(kept),
        out_specs=VMEM,
        out_shape=jax.ShapeDtypeStruct((fronts, panel + EXTRA, width), bf16),
        scratch_shapes=[
            pltpu.VMEM((rows, width), bf16),
            pltpu.VMEM((2, rows, width), bf16),
            pltpu.SemaphoreType.DMA((2,)),
        ],
        compiler_params=params(),
    )(where, exchange(sent), after, *kept)
    home = lax.all_to_all(homeward, ("parity", "half"), 0, 0, tiled=True)
    values = jnp.sum(home[:, panel : panel + 3, 0].astype(f32), axis=1)
    return home[None, :, :panel], values[:, None]


def solution(mesh):
    links, peers = mesh.devices.shape
    devices = mesh.devices.reshape(links // 2, 2, 2, peers // 2)
    chain, bond = ("pair", "parity"), ("half", "member")
    placed = (P(chain, bond, None, None), P(None, bond, None), P(), P(), P(), P())
    return jax.shard_map(
        on_device,
        mesh=Mesh(devices, chain + bond),
        in_specs=placed,
        out_specs=(P(chain, None, bond, None), P(None, chain)),
        check_vma=False,
    )
```

```python
import functools
import math

import jax
import jax.numpy as jnp
from jax import lax
from jax.experimental import pallas as pl
from jax.experimental.pallas import tpu as pltpu
from jax.sharding import Mesh
from jax.sharding import PartitionSpec as P

EXTRA = 16
MIB = 1 << 20
COLS = 256


def two_parts(value):
    high = value.astype(jnp.bfloat16).astype(jnp.float32)
    return jnp.concatenate([high, value - high], axis=0).astype(jnp.bfloat16)


def columns(tensor_ref, t, c):
    if len(tensor_ref.shape) == 4:
        return tensor_ref[:, t, :, c * COLS : (c + 1) * COLS].reshape(-1, COLS)
    per = tensor_ref.shape[5] // COLS
    at = c % per * COLS
    return tensor_ref[:, c // per, :, t, :, at : at + COLS].reshape(-1, COLS)


def block(tensor_ref, d, s, c):
    if len(tensor_ref.shape) == 4:
        return tensor_ref[d, s, :, c * COLS : (c + 1) * COLS].reshape(-1, COLS)
    per = tensor_ref.shape[5] // COLS
    at = c % per * COLS
    return tensor_ref[d // 2, c // per, d % 2, s, :, at : at + COLS].reshape(-1, COLS)


def spread(slot, where_ref, mix_ref, look_ref, env, tensor_ref, out_ref, arrived=None):
    width = env.shape[1]
    phys = mix_ref.shape[1]
    panel = env.shape[0] // 2
    half = width // panel // 2
    mem = where_ref[0]
    total = jnp.zeros((1, 128), jnp.float32)
    for c in range(width // COLS):
        if arrived is not None:
            arrived[c]()
        prods = [
            jnp.dot(env, columns(tensor_ref, t, c), preferred_element_type=jnp.float32)
            for t in range(phys)
        ]
        for s in range(phys):
            own = jnp.concatenate(
                [block(tensor_ref, h * half + mem, s, c) for h in range(2)], axis=0
            ).astype(jnp.float32)
            seen = own * sum(look_ref[slot, s, t] * prods[t] for t in range(phys))
            line = jnp.sum(seen, axis=0, keepdims=True)
            total += sum(line[:, b : b + 128] for b in range(0, COLS, 128))
        mixed = [sum(mix_ref[slot, s, t] * prods[t] for t in range(phys)) for s in range(phys)]
        tall = jnp.concatenate(
            [mixed[s][h * panel : (h + 1) * panel] for h in range(2) for s in range(phys)], axis=0
        )
        turned = tall.astype(jnp.bfloat16).T.reshape(COLS // panel, panel, 2 * phys * panel)
        first = c * (COLS // panel)
        h, first = first // half, first % half
        out_ref[first : first + COLS // panel, h * panel : (h + 1) * panel, :] = turned
    return total


def gather(moved_ref, tensor_ref, env_ref):
    rows, width = env_ref.shape
    half = moved_ref.shape[0]
    if moved_ref.shape[1] < rows:
        left = [
            jnp.concatenate([moved_ref[g], moved_ref[g + 1]], axis=0) for g in range(0, half, 2)
        ]
    else:
        left = [moved_ref[g, :rows] for g in range(half)]
    left = jnp.concatenate(left, axis=1)
    for c in range(width // COLS):
        right = jnp.concatenate(
            [
                block(tensor_ref, h * half + g, slice(None), c)
                for g in range(half)
                for h in range(2)
            ],
            axis=0,
        )
        env_ref[:, c * COLS : (c + 1) * COLS] = jnp.dot(
            left, right, preferred_element_type=jnp.float32
        ).astype(jnp.bfloat16)


def chip_of(side, where_ref, at, m, k):
    y, x = where_ref[2], where_ref[3]
    along = lax.rem(y + side - jnp.where(at == 0, m, k), side)
    across = lax.rem(x + side - jnp.where(at == 0, k, m), side)
    return along * side + across


def lay(side, where_ref, pieces, tensor_ref, sems):
    copies = []
    for i, ref in enumerate(pieces):
        at = where_ref[4] if i < side else 1 - where_ref[4]
        for k in range(side):
            place = tensor_ref.at[chip_of(side, where_ref, at, i % side, k), at]
            copies.append(pltpu.make_async_copy(ref.at[k], place, sems.at[i, k]))
    for copy in copies:
        copy.start()
    return copies


def lay_kernel(side, where_ref, *refs):
    for copy in lay(side, where_ref, refs[:-2], refs[-2], refs[-1]):
        copy.wait()


def pieces_kernel(side, where_ref, moved_ref, *refs):
    pieces, (env_ref, tensor, sems) = refs[:-3], refs[-3:]
    copies = lay(side, where_ref, pieces, tensor, sems)
    chips, wide = tensor.shape[0], tensor.shape[5]
    left = jnp.concatenate(
        [
            jnp.concatenate([moved_ref[g], moved_ref[g + 1]], axis=0) for g in range(0, chips, 2)
        ],
        axis=1,
    )
    for part in range(2):
        at = where_ref[4] if part == 0 else 1 - where_ref[4]
        for copy in copies[part * side * side : (part + 1) * side * side]:
            copy.wait()
        for c in range(wide // COLS):
            cols = slice(c * COLS, (c + 1) * COLS)
            right = jnp.concatenate(
                [
                    tensor[(h * chips + g) // 2, at, g % 2, :, :, cols].reshape(-1, COLS)
                    for g in range(chips)
                    for h in range(2)
                ],
                axis=0,
            )
            place = pl.ds(pl.multiple_of(at * wide + c * COLS, COLS), COLS)
            env_ref[:, place] = jnp.dot(
                left, right, preferred_element_type=jnp.float32
            ).astype(jnp.bfloat16)


def stream_kernel(
    now, where_ref, mix_ref, look_ref, env_ref, tensor_ref, seen_ref, out_ref, new_ref, held, sems
):
    copies = []
    for c in range(held.shape[3] // COLS):
        cols = pl.ds(c * COLS, COLS)
        copies.append(
            pltpu.make_async_copy(
                tensor_ref.at[:, :, :, cols], held.at[:, :, :, cols], sems.at[c]
            )
        )
        copies[-1].start()
    arrived = [copy.wait for copy in copies]
    total = spread(1, where_ref, mix_ref, look_ref, env_ref[...], held, out_ref, arrived)
    new_ref[0] = seen_ref[0]
    first_row = lax.broadcasted_iota(jnp.int32, new_ref.shape[1:], 0) == 0
    new_ref[1] = jnp.where(first_row, jnp.broadcast_to(total, new_ref.shape[1:]), 0.0)


def load(side, where_ref, pieces, tensor_ref, sems):
    blocks = []
    for c in range(tensor_ref.shape[4] // COLS):
        cols = pl.ds(c * COLS, COLS)
        copies = []
        for m, ref in enumerate(pieces):
            for k in range(side):
                chip = chip_of(side, where_ref, where_ref[4], m, k)
                copies.append(
                    pltpu.make_async_copy(
                        ref.at[k, :, :, :, cols], tensor_ref.at[chip, :, :, :, cols], sems.at[c, m, k]
                    )
                )
        for copy in copies:
            copy.start()
        blocks.append(copies)
    return blocks


def start_kernel(side, where_ref, mix_ref, look_ref, env_ref, twin_ref, *refs):
    pieces, (out_ref, new_ref, tensor, sems) = refs[:-4], refs[-4:]
    core = where_ref[4]
    blocks = load(side, where_ref, pieces, tensor, sems)
    own, twin = env_ref[...], twin_ref[...]
    env = jnp.concatenate(
        [jnp.where(core == 0, own, twin), jnp.where(core == 0, twin, own)], axis=0
    )
    chips, _, phys, panel, wide = tensor.shape
    mem = where_ref[0] // 2
    total = jnp.zeros((1, 128), jnp.float32)
    for c, copies in enumerate(blocks):
        for copy in copies:
            copy.wait()
        cols = slice(c * COLS, (c + 1) * COLS)
        prods = [
            jnp.dot(
                env, tensor[:, :, t, :, cols].reshape(-1, COLS), preferred_element_type=jnp.float32
            )
            for t in range(phys)
        ]
        for s in range(phys):
            rows = [tensor[h * (chips // 2) + mem, o, s, :, cols] for o in range(2) for h in range(2)]
            seen = jnp.concatenate(rows, axis=0).astype(jnp.float32)
            seen = seen * sum(look_ref[0, s, t] * prods[t] for t in range(phys))
            line = jnp.sum(seen, axis=0, keepdims=True)
            total += sum(line[:, b : b + 128] for b in range(0, COLS, 128))
        mixed = [sum(mix_ref[0, s, t] * prods[t] for t in range(phys)) for s in range(phys)]
        tall = [mixed[s][q * panel : (q + 1) * panel] for q in range(4) for s in range(phys)]
        turned = jnp.concatenate(tall, axis=0).astype(jnp.bfloat16).T
        per = COLS // panel
        out_ref[c * per : (c + 1) * per] = turned.reshape(per, panel, 4 * phys * panel)
    first_row = lax.broadcasted_iota(jnp.int32, new_ref.shape[1:], 0) == 0
    total = jnp.where(first_row, jnp.broadcast_to(total, new_ref.shape[1:]), 0.0)
    new_ref[...] = jnp.broadcast_to(total[None], new_ref.shape)


def spread_plain(slot, mix_ref, bank_ref, env, tensor_ref, out_ref):
    width = env.shape[1]
    phys = bank_ref.shape[1]
    panel = env.shape[0] // 2
    half = width // panel // 2
    total = jnp.zeros((8, 128), jnp.float32)
    for c in range(width // COLS):
        prods = [
            jnp.dot(env, columns(tensor_ref, t, c), preferred_element_type=jnp.float32)
            for t in range(phys)
        ]
        seen = sum(bank_ref[slot, t, :, c * COLS : (c + 1) * COLS] * prods[t] for t in range(phys))
        seen = jnp.sum(seen.reshape(-1, 8, COLS), axis=0)
        total += sum(seen[:, b : b + 128] for b in range(0, COLS, 128))

        def factor(s, t):
            row = slot * phys * phys + s * phys + t
            return mix_ref[row : row + 1]

        mixed = [sum(factor(s, t) * prods[t] for t in range(phys)) for s in range(phys)]
        tall = jnp.concatenate(
            [mixed[s][h * panel : (h + 1) * panel] for h in range(2) for s in range(phys)], axis=0
        )
        turned = tall.astype(jnp.bfloat16).T.reshape(COLS // panel, panel, 2 * phys * panel)
        first = c * (COLS // panel)
        h, first = first // half, first % half
        out_ref[first : first + COLS // panel, h * panel : (h + 1) * panel, :] = turned
    return total


def first_kernel(now, pair_ref, mix_ref, bank_ref, env_ref, tensor_ref, seen_ref, out_ref, new_ref):
    total = spread_plain(0, mix_ref, bank_ref, env_ref[...], tensor_ref, out_ref)
    new_ref[0] = jnp.where(pair_ref[...] == now, total, seen_ref[0])
    new_ref[1] = seen_ref[1]


def middle_kernel(
    now, pair_ref, mix_ref, bank_ref, moved_ref, old_ref, tensor_ref, seen_ref, out_ref, new_ref, env_ref
):
    gather(moved_ref, old_ref, env_ref)
    total = spread_plain(1, mix_ref, bank_ref, env_ref[...], tensor_ref, out_ref)
    new_ref[0] = seen_ref[0]
    new_ref[1] = jnp.where(pair_ref[...] == now, total, seen_ref[1])


def end_kernel(
    now, pair_ref, mix_ref, bank_ref, moved_ref, old_ref, tensor_ref, seen_ref, out_ref, env_ref
):
    gather(moved_ref, old_ref, env_ref)
    total = spread_plain(1, mix_ref, bank_ref, env_ref[...], tensor_ref, out_ref)
    rows, lanes = env_ref.shape[0], out_ref.shape[2]
    odd = jnp.where(pair_ref[...] == now, total, seen_ref[1])
    extra = jnp.concatenate([two_parts(v) for v in (seen_ref[0], odd)], axis=1)
    out_ref[:, rows:, :] = jnp.broadcast_to(extra[None], (out_ref.shape[0], EXTRA, lanes))


def bank_kernel(where_ref, look_ref, *refs):
    tensors, bank_ref = refs[:-1], refs[-1]
    slots, phys, rows, width = bank_ref.shape
    half = width // rows
    for slot, ref in enumerate(tensors):
        for c in range(width // COLS):
            own = [
                jnp.concatenate(
                    [block(ref, h * half + where_ref[0], s, c) for h in range(2)], axis=0
                ).astype(jnp.float32)
                for s in range(phys)
            ]
            for t in range(phys):
                bank_ref[slot, t, :, c * COLS : (c + 1) * COLS] = sum(
                    look_ref[slot, s, t] * own[s] for s in range(phys)
                )


def pick_kernel(pair_ref, *refs):
    kept, outs = refs[:-2], refs[-2:]
    count = len(kept) // 2
    pair = pair_ref[:1, :1]
    for q in range(2):
        value = kept[q * count][...]
        for p in range(1, count):
            value = jnp.where(pair == p, kept[q * count + p][...], value)
        outs[q][...] = value


def second_kernel(moved_ref, tensor_ref, env_ref):
    gather(moved_ref, tensor_ref, env_ref)


def home_kernel(now, pair_ref, moved_ref, tensor_ref, even_ref, odd_ref, six_ref, out_ref, env):
    gather(moved_ref, tensor_ref, env)
    rows = env.shape[0]
    panel = rows // 2
    here = pair_ref[:1, :1] == now
    values = jnp.sum(moved_ref[:, rows:].astype(jnp.float32), axis=0)
    for q, (kept, last) in enumerate(((even_ref, six_ref), (odd_ref, env))):
        result = jnp.where(here, last[...], kept[...])
        value = values[:, q * 128 : (q + 1) * 128]
        extra = two_parts(value[:8] + value[8:])
        for h in range(2):
            out_ref[2 * q + h, :panel] = result[h * panel : (h + 1) * panel]
            out_ref[2 * q + h, panel:] = jnp.zeros_like(out_ref[0, panel:])
            out_ref[2 * q + h, panel:, :128] = extra


def mix_kernel(
    width, where_ref, site_ref, kind_ref, operators_ref, probe_ref, mix_ref, look_ref, factor_ref, pair_ref
):
    pair, front = where_ref[1], where_ref[6]
    pair_ref[...] = jnp.zeros_like(pair_ref) + pair
    kind, site = kind_ref[front], site_ref[front]
    phys = probe_ref.shape[0]
    scale = 1.0 / math.sqrt(width)
    for slot in range(2):
        for s in range(phys):
            for t in range(phys):
                row, col = (s, t) if slot == 0 else (t, s)
                own = 1.0 if s == t else 0.0
                factor = jnp.where(site == 2 * pair + slot, operators_ref[kind, row, col], own)
                mix_ref[slot, s, t] = factor
                line = (slot * phys + s) * phys + t
                factor_ref[line : line + 1] = jnp.zeros((1, factor_ref.shape[1]), jnp.float32) + factor
                look_ref[slot, s, t] = probe_ref[row, col] * scale


def cut_kernel(
    where_ref, mine_ref, near_ref, start_ref, other_ref, keep_ref, give_ref, env_ref, sem
):
    core, half, front, parity = where_ref[4], where_ref[5], where_ref[6], where_ref[7]
    panel = other_ref.shape[0]
    copy = pltpu.make_async_copy(
        start_ref.at[front], env_ref.at[pl.ds(pl.multiple_of(half * panel, panel), panel)], sem.at[0]
    )
    copy.start()
    env_ref[pl.ds(pl.multiple_of((1 - half) * panel, panel), panel)] = other_ref[...]
    wide = keep_ref.shape[2]
    mine, near = mine_ref[...], near_ref[...]
    begun = jnp.where(parity == 0, mine, near)
    low, high = begun[..., :wide], begun[..., wide:]
    keep_ref[...] = jnp.where(core == 0, low, high)
    give_ref[...] = jnp.where(core == 0, high, low)
    copy.wait()


SMEM = pl.BlockSpec(memory_space=pltpu.SMEM)
VMEM = pl.BlockSpec(memory_space=pltpu.VMEM)
ANY = pl.BlockSpec(memory_space=pl.ANY)
HBM = pl.BlockSpec(memory_space=pltpu.HBM)


def params():
    return pltpu.CompilerParams(vmem_limit_bytes=16 * MIB)


def shifts(side, by, first):
    pairs = []
    for y in range(side):
        for x in range(side):
            for core in range(2):
                across = (core == 0) == first
                to = y * side + (x + by) % side if across else (y + by) % side * side + x
                pairs.append(((y * side + x) * 2 + core, to * 2 + core))
    return pairs


def in_hbm(arrays):
    return [pltpu.with_memory_space_constraint(a, pltpu.HBM) for a in arrays]


def first_ring(keep, give, core, side):
    bond = ("half", "member")
    other = lax.ppermute(give, bond, twins(side))
    chip = jnp.where(core == 0, jnp.stack([keep, other]), jnp.stack([other, keep]))
    return jnp.stack([chip] + [lax.ppermute(chip, bond, shifts(side, k, True)) for k in range(1, side)])


def second_ring(row, side):
    bond = ("half", "member")
    return [row] + [lax.ppermute(row, bond, shifts(side, m, False)) for m in range(1, side)]


def swap_cores(pieces, side):
    return [lax.ppermute(p, ("half", "member"), twins(side)) for p in pieces]


def twins(side):
    return [(i, i ^ 1) for i in range(2 * side * side)]


def on_device(site_tensors, start_env, operators, op_site, op_kind, probe):
    fronts, panel, width = start_env.shape
    phys = site_tensors.shape[2]
    kinds = operators.shape[0]
    pairs = lax.axis_size("pair")
    pair = lax.axis_index("pair")
    parity = lax.axis_index("parity")
    half = lax.axis_index("half")
    member = lax.axis_index("member")
    members = lax.axis_size("member")
    side = math.isqrt(members)
    rows = 2 * panel
    lanes = 2 * phys * panel
    f32 = jnp.float32
    bf16 = jnp.bfloat16
    core = member % 2
    chip = half * (members // 2) + member // 2
    front = 2 * parity + half
    where = jnp.stack([member, pair, chip // side, chip % side, core, half, front, parity]).astype(jnp.int32)

    mine = jnp.swapaxes(site_tensors[0], 0, 1)
    near = lax.ppermute(mine, "parity", [(0, 1), (1, 0)])
    given = lax.dynamic_index_in_dim(start_env, 2 * parity + 1 - half, 0, keepdims=False)
    other = lax.ppermute(given, "half", [(0, 1), (1, 0)])
    env_shape = jax.ShapeDtypeStruct((rows, width), bf16)
    square = jax.ShapeDtypeStruct((2, phys, phys), f32)
    part = jax.ShapeDtypeStruct((phys, panel, width // 2), bf16)
    bond = ("half", "member")
    mixes, looks, factors, pairs_here = pl.pallas_call(
        functools.partial(mix_kernel, width),
        in_specs=[SMEM] * 5,
        out_specs=[SMEM] * 2 + [VMEM] * 2,
        out_shape=[
            square,
            square,
            jax.ShapeDtypeStruct((2 * phys * phys, COLS), f32),
            jax.ShapeDtypeStruct((8, 128), jnp.int32),
        ],
        compiler_params=params(),
    )(where, op_site, op_kind, operators, probe)
    where, other, mine, near, mixes, looks, factors, pairs_here = lax.optimization_barrier(
        (where, other, mine, near, mixes, looks, factors, pairs_here)
    )
    small = (where, mixes, looks)
    after = lax.all_gather(jnp.where(parity == 0, near, mine), bond, axis=0)
    keep, give, env = pl.pallas_call(
        cut_kernel,
        in_specs=[SMEM] + [VMEM] * 2 + [ANY, VMEM],
        out_specs=[VMEM] * 3,
        out_shape=[part, part, env_shape],
        scratch_shapes=[pltpu.SemaphoreType.DMA((1,))],
        compiler_params=params(),
    )(where, mine, near, start_env, other)
    twin = lax.ppermute(env, bond, twins(side))
    row = first_ring(keep, give, core, side)
    row, twin = lax.optimization_barrier((row, twin))
    pieces = second_ring(row, side)
    swapped = swap_cores(pieces, side)

    def sent_shape(extra):
        return jax.ShapeDtypeStruct((members, rows + extra, lanes), bf16)

    seen_shape = jax.ShapeDtypeStruct((2, 8, 128), f32)

    def exchange(sent):
        return lax.all_to_all(sent, "member", 0, 0, tiled=True)

    sent, seen = pl.pallas_call(
        functools.partial(start_kernel, side),
        in_specs=[SMEM] * 3 + [VMEM] * 2 + [HBM] * side,
        out_specs=[VMEM] * 2,
        out_shape=[jax.ShapeDtypeStruct((members, panel, 2 * lanes), bf16), seen_shape],
        scratch_shapes=[
            pltpu.VMEM((side * side, 2, phys, panel, width // 2), bf16),
            pltpu.SemaphoreType.DMA((width // 2 // COLS, side, side)),
        ],
        compiler_params=params(),
    )(*small, env, twin, *in_hbm(pieces))
    moved = exchange(sent)
    whole = (side * side, 2, 2, phys, panel, width // 2)
    lay_sems = pltpu.SemaphoreType.DMA((2 * side, side))
    everything = pieces + swapped
    env = pl.pallas_call(
        functools.partial(pieces_kernel, side),
        in_specs=[SMEM, VMEM] + [HBM] * (2 * side),
        out_specs=VMEM,
        out_shape=env_shape,
        scratch_shapes=[pltpu.VMEM(whole, bf16), lay_sems],
        compiler_params=params(),
    )(where, moved, *in_hbm(everything))
    evens, odds = [env], []
    env, after = lax.optimization_barrier((env, after))
    sent, seen = pl.pallas_call(
        functools.partial(stream_kernel, 0),
        in_specs=[SMEM] * 3 + [VMEM, HBM, VMEM],
        out_specs=[VMEM] * 2,
        out_shape=[sent_shape(0), seen_shape],
        scratch_shapes=[
            pltpu.VMEM(after.shape, bf16),
            pltpu.SemaphoreType.DMA((width // COLS,)),
        ],
        compiler_params=params(),
    )(*small, env, *in_hbm([after]), seen)
    after = pltpu.with_memory_space_constraint(after, pltpu.VMEM)
    before = None
    for now in range(pairs - 1):
        if now > 0:
            sent, seen, env = pl.pallas_call(
                functools.partial(middle_kernel, now),
                in_specs=[VMEM] * 7,
                out_specs=[VMEM] * 3,
                out_shape=[sent_shape(0), seen_shape, env_shape],
                compiler_params=params(),
            )(*vectors, exchange(sent), before, after, seen)
            evens.append(env)
        env = pl.pallas_call(
            second_kernel,
            in_specs=[VMEM] * 2,
            out_specs=VMEM,
            out_shape=env_shape,
            compiler_params=params(),
        )(exchange(sent), after)
        odds.append(env)
        if now == 0:
            env, everything = lax.optimization_barrier((env, everything))
            before = pl.pallas_call(
                functools.partial(lay_kernel, side),
                in_specs=[SMEM] + [HBM] * (2 * side),
                out_specs=ANY,
                out_shape=jax.ShapeDtypeStruct(whole, bf16),
                scratch_shapes=[lay_sems],
                compiler_params=params(),
            )(where, *in_hbm(everything))
            before = pltpu.with_memory_space_constraint(before, pltpu.VMEM)
            bank = pl.pallas_call(
                bank_kernel,
                in_specs=[SMEM] * 2 + [VMEM] * 2,
                out_specs=VMEM,
                out_shape=jax.ShapeDtypeStruct((2, phys, rows, width), f32),
                compiler_params=params(),
            )(where, looks, before, after)
            vectors = (pairs_here, factors, bank)
        if now == pairs - 2:
            env, *kept = lax.optimization_barrier((env, *evens, *odds))
            picked = pl.pallas_call(
                pick_kernel,
                in_specs=[VMEM] * (1 + len(kept)),
                out_specs=[VMEM] * 2,
                out_shape=[env_shape] * 2,
                compiler_params=params(),
            )(pairs_here, *kept)
        env = lax.ppermute(env, "pair", [(now, now + 1)])
        if now == pairs - 2:
            env, picked = lax.optimization_barrier((env, picked))
        sent, seen = pl.pallas_call(
            functools.partial(first_kernel, now + 1),
            in_specs=[VMEM] * 6,
            out_specs=[VMEM] * 2,
            out_shape=[sent_shape(0), seen_shape],
            compiler_params=params(),
        )(*vectors, env, before, seen)
    moved = exchange(sent)
    sent, env = pl.pallas_call(
        functools.partial(end_kernel, pairs - 1),
        in_specs=[VMEM] * 7,
        out_specs=[VMEM] * 2,
        out_shape=[sent_shape(EXTRA), env_shape],
        compiler_params=params(),
    )(*vectors, moved, before, after, seen)
    homeward = pl.pallas_call(
        functools.partial(home_kernel, pairs - 1),
        in_specs=[VMEM] * 6,
        out_specs=VMEM,
        out_shape=jax.ShapeDtypeStruct((fronts, panel + EXTRA, width), bf16),
        scratch_shapes=[pltpu.VMEM((rows, width), bf16)],
        compiler_params=params(),
    )(pairs_here, exchange(sent), after, *picked, env)
    home = lax.all_to_all(homeward, ("parity", "half"), 0, 0, tiled=True)
    values = jnp.sum(home[:, panel:, :128].astype(f32), axis=(1, 2))
    return home[None, :, :panel], values[:, None]


def solution(mesh):
    links, peers = mesh.devices.shape
    devices = mesh.devices.reshape(links // 2, 2, 2, peers // 2)
    chain, bond = ("pair", "parity"), ("half", "member")
    placed = (P(chain, bond, None, None), P(None, bond, None), P(), P(), P(), P())
    return jax.shard_map(
        on_device,
        mesh=Mesh(devices, chain + bond),
        in_specs=placed,
        out_specs=(P(chain, None, bond, None), P(None, chain)),
        check_vma=False,
    )
```

```python
import functools
import math

import jax
import jax.numpy as jnp
from jax import lax
from jax.experimental import pallas as pl
from jax.experimental.pallas import tpu as pltpu
from jax.sharding import Mesh
from jax.sharding import PartitionSpec as P

EXTRA = 16
MIB = 1 << 20
COLS = 256


def two_parts(value):
    high = value.astype(jnp.bfloat16).astype(jnp.float32)
    return jnp.concatenate([high, value - high], axis=0).astype(jnp.bfloat16)


def columns(tensor_ref, t, c):
    if len(tensor_ref.shape) == 4:
        return tensor_ref[:, t, :, c * COLS : (c + 1) * COLS].reshape(-1, COLS)
    per = tensor_ref.shape[5] // COLS
    at = c % per * COLS
    return tensor_ref[:, c // per, :, t, :, at : at + COLS].reshape(-1, COLS)


def block(tensor_ref, d, s, c):
    if len(tensor_ref.shape) == 4:
        return tensor_ref[d, s, :, c * COLS : (c + 1) * COLS].reshape(-1, COLS)
    per = tensor_ref.shape[5] // COLS
    at = c % per * COLS
    return tensor_ref[d // 2, c // per, d % 2, s, :, at : at + COLS].reshape(-1, COLS)


def spread(slot, where_ref, mix_ref, look_ref, env, tensor_ref, out_ref, arrived=None):
    width = env.shape[1]
    phys = mix_ref.shape[1]
    panel = env.shape[0] // 2
    half = width // panel // 2
    mem = where_ref[0]
    total = jnp.zeros((1, 128), jnp.float32)
    for c in range(width // COLS):
        if arrived is not None:
            arrived[c]()
        prods = [
            jnp.dot(env, columns(tensor_ref, t, c), preferred_element_type=jnp.float32)
            for t in range(phys)
        ]
        for s in range(phys):
            own = jnp.concatenate(
                [block(tensor_ref, h * half + mem, s, c) for h in range(2)], axis=0
            ).astype(jnp.float32)
            seen = own * sum(look_ref[slot, s, t] * prods[t] for t in range(phys))
            line = jnp.sum(seen, axis=0, keepdims=True)
            total += sum(line[:, b : b + 128] for b in range(0, COLS, 128))
        mixed = [sum(mix_ref[slot, s, t] * prods[t] for t in range(phys)) for s in range(phys)]
        tall = jnp.concatenate(
            [mixed[s][h * panel : (h + 1) * panel] for h in range(2) for s in range(phys)], axis=0
        )
        turned = tall.astype(jnp.bfloat16).T.reshape(COLS // panel, panel, 2 * phys * panel)
        first = c * (COLS // panel)
        h, first = first // half, first % half
        out_ref[first : first + COLS // panel, h * panel : (h + 1) * panel, :] = turned
    return total


def gather(moved_ref, tensor_ref, env_ref):
    rows, width = env_ref.shape
    half = moved_ref.shape[0]
    if moved_ref.shape[1] < rows:
        left = [
            jnp.concatenate([moved_ref[g], moved_ref[g + 1]], axis=0) for g in range(0, half, 2)
        ]
    else:
        left = [moved_ref[g, :rows] for g in range(half)]
    left = jnp.concatenate(left, axis=1)
    for c in range(width // COLS):
        right = jnp.concatenate(
            [
                block(tensor_ref, h * half + g, slice(None), c)
                for g in range(half)
                for h in range(2)
            ],
            axis=0,
        )
        env_ref[:, c * COLS : (c + 1) * COLS] = jnp.dot(
            left, right, preferred_element_type=jnp.float32
        ).astype(jnp.bfloat16)


def chip_of(side, where_ref, at, m, k):
    y, x = where_ref[2], where_ref[3]
    along = lax.rem(y + side - jnp.where(at == 0, m, k), side)
    across = lax.rem(x + side - jnp.where(at == 0, k, m), side)
    return along * side + across


def lay(side, where_ref, pieces, tensor_ref, sems):
    copies = []
    for i, ref in enumerate(pieces):
        at = where_ref[4] if i < side else 1 - where_ref[4]
        for k in range(side):
            place = tensor_ref.at[chip_of(side, where_ref, at, i % side, k), at]
            copies.append(pltpu.make_async_copy(ref.at[k], place, sems.at[i, k]))
    for copy in copies:
        copy.start()
    return copies


def lay_kernel(side, where_ref, *refs):
    for copy in lay(side, where_ref, refs[:-2], refs[-2], refs[-1]):
        copy.wait()


def pieces_kernel(side, where_ref, moved_ref, *refs):
    pieces, (env_ref, tensor, sems) = refs[:-3], refs[-3:]
    copies = lay(side, where_ref, pieces, tensor, sems)
    chips, wide = tensor.shape[0], tensor.shape[5]
    left = jnp.concatenate(
        [
            jnp.concatenate([moved_ref[g], moved_ref[g + 1]], axis=0) for g in range(0, chips, 2)
        ],
        axis=1,
    )
    for part in range(2):
        at = where_ref[4] if part == 0 else 1 - where_ref[4]
        for copy in copies[part * side * side : (part + 1) * side * side]:
            copy.wait()
        for c in range(wide // COLS):
            cols = slice(c * COLS, (c + 1) * COLS)
            right = jnp.concatenate(
                [
                    tensor[(h * chips + g) // 2, at, g % 2, :, :, cols].reshape(-1, COLS)
                    for g in range(chips)
                    for h in range(2)
                ],
                axis=0,
            )
            place = pl.ds(pl.multiple_of(at * wide + c * COLS, COLS), COLS)
            env_ref[:, place] = jnp.dot(
                left, right, preferred_element_type=jnp.float32
            ).astype(jnp.bfloat16)


def stream_kernel(
    now, where_ref, mix_ref, look_ref, env_ref, tensor_ref, seen_ref, out_ref, new_ref, held, sems
):
    copies = []
    for c in range(held.shape[3] // COLS):
        cols = pl.ds(c * COLS, COLS)
        copies.append(
            pltpu.make_async_copy(
                tensor_ref.at[:, :, :, cols], held.at[:, :, :, cols], sems.at[c]
            )
        )
        copies[-1].start()
    arrived = [copy.wait for copy in copies]
    total = spread(1, where_ref, mix_ref, look_ref, env_ref[...], held, out_ref, arrived)
    new_ref[0] = seen_ref[0]
    first_row = lax.broadcasted_iota(jnp.int32, new_ref.shape[1:], 0) == 0
    new_ref[1] = jnp.where(first_row, jnp.broadcast_to(total, new_ref.shape[1:]), 0.0)


def load(side, where_ref, pieces, tensor_ref, sems):
    blocks = []
    for c in range(tensor_ref.shape[4] // COLS):
        cols = pl.ds(c * COLS, COLS)
        copies = []
        for m, ref in enumerate(pieces):
            for k in range(side):
                chip = chip_of(side, where_ref, where_ref[4], m, k)
                copies.append(
                    pltpu.make_async_copy(
                        ref.at[k, :, :, :, cols], tensor_ref.at[chip, :, :, :, cols], sems.at[c, m, k]
                    )
                )
        for copy in copies:
            copy.start()
        blocks.append(copies)
    return blocks


def start_kernel(side, where_ref, mix_ref, look_ref, env_ref, twin_ref, *refs):
    pieces, (out_ref, new_ref, tensor, sems) = refs[:-4], refs[-4:]
    core = where_ref[4]
    blocks = load(side, where_ref, pieces, tensor, sems)
    own, twin = env_ref[...], twin_ref[...]
    env = jnp.concatenate(
        [jnp.where(core == 0, own, twin), jnp.where(core == 0, twin, own)], axis=0
    )
    chips, _, phys, panel, wide = tensor.shape
    mem = where_ref[0] // 2
    total = jnp.zeros((1, 128), jnp.float32)
    for c, copies in enumerate(blocks):
        for copy in copies:
            copy.wait()
        cols = slice(c * COLS, (c + 1) * COLS)
        prods = [
            jnp.dot(
                env, tensor[:, :, t, :, cols].reshape(-1, COLS), preferred_element_type=jnp.float32
            )
            for t in range(phys)
        ]
        for s in range(phys):
            rows = [tensor[h * (chips // 2) + mem, o, s, :, cols] for o in range(2) for h in range(2)]
            seen = jnp.concatenate(rows, axis=0).astype(jnp.float32)
            seen = seen * sum(look_ref[0, s, t] * prods[t] for t in range(phys))
            line = jnp.sum(seen, axis=0, keepdims=True)
            total += sum(line[:, b : b + 128] for b in range(0, COLS, 128))
        mixed = [sum(mix_ref[0, s, t] * prods[t] for t in range(phys)) for s in range(phys)]
        tall = [mixed[s][q * panel : (q + 1) * panel] for q in range(4) for s in range(phys)]
        turned = jnp.concatenate(tall, axis=0).astype(jnp.bfloat16).T
        per = COLS // panel
        out_ref[c * per : (c + 1) * per] = turned.reshape(per, panel, 4 * phys * panel)
    first_row = lax.broadcasted_iota(jnp.int32, new_ref.shape[1:], 0) == 0
    total = jnp.where(first_row, jnp.broadcast_to(total, new_ref.shape[1:]), 0.0)
    new_ref[...] = jnp.broadcast_to(total[None], new_ref.shape)


def spread_plain(slot, mix_ref, bank_ref, env, tensor_ref, out_ref):
    width = env.shape[1]
    phys = bank_ref.shape[1]
    panel = env.shape[0] // 2
    half = width // panel // 2
    total = jnp.zeros((8, 128), jnp.float32)
    for c in range(width // COLS):
        prods = [
            jnp.dot(env, columns(tensor_ref, t, c), preferred_element_type=jnp.float32)
            for t in range(phys)
        ]
        seen = sum(bank_ref[slot, t, :, c * COLS : (c + 1) * COLS] * prods[t] for t in range(phys))
        seen = jnp.sum(seen.reshape(-1, 8, COLS), axis=0)
        total += sum(seen[:, b : b + 128] for b in range(0, COLS, 128))

        def factor(s, t):
            row = slot * phys * phys + s * phys + t
            return mix_ref[row : row + 1]

        mixed = [sum(factor(s, t) * prods[t] for t in range(phys)) for s in range(phys)]
        tall = jnp.concatenate(
            [mixed[s][h * panel : (h + 1) * panel] for h in range(2) for s in range(phys)], axis=0
        )
        turned = tall.astype(jnp.bfloat16).T.reshape(COLS // panel, panel, 2 * phys * panel)
        first = c * (COLS // panel)
        h, first = first // half, first % half
        out_ref[first : first + COLS // panel, h * panel : (h + 1) * panel, :] = turned
    return total


def first_kernel(now, pair_ref, mix_ref, bank_ref, env_ref, tensor_ref, seen_ref, out_ref, new_ref):
    total = spread_plain(0, mix_ref, bank_ref, env_ref[...], tensor_ref, out_ref)
    new_ref[0] = jnp.where(pair_ref[...] == now, total, seen_ref[0])
    new_ref[1] = seen_ref[1]


def middle_kernel(
    now, pair_ref, mix_ref, bank_ref, moved_ref, old_ref, tensor_ref, seen_ref, out_ref, new_ref, env_ref
):
    gather(moved_ref, old_ref, env_ref)
    total = spread_plain(1, mix_ref, bank_ref, env_ref[...], tensor_ref, out_ref)
    new_ref[0] = seen_ref[0]
    new_ref[1] = jnp.where(pair_ref[...] == now, total, seen_ref[1])


def end_kernel(
    now, pair_ref, mix_ref, bank_ref, moved_ref, old_ref, tensor_ref, seen_ref, out_ref, env_ref
):
    gather(moved_ref, old_ref, env_ref)
    total = spread_plain(1, mix_ref, bank_ref, env_ref[...], tensor_ref, out_ref)
    rows, lanes = env_ref.shape[0], out_ref.shape[2]
    odd = jnp.where(pair_ref[...] == now, total, seen_ref[1])
    extra = jnp.concatenate([two_parts(v) for v in (seen_ref[0], odd)], axis=1)
    out_ref[:, rows:, :] = jnp.broadcast_to(extra[None], (out_ref.shape[0], EXTRA, lanes))


def bank_kernel(where_ref, look_ref, *refs):
    tensors, bank_ref = refs[:-1], refs[-1]
    slots, phys, rows, width = bank_ref.shape
    half = width // rows
    for slot, ref in enumerate(tensors):
        for c in range(width // COLS):
            own = [
                jnp.concatenate(
                    [block(ref, h * half + where_ref[0], s, c) for h in range(2)], axis=0
                ).astype(jnp.float32)
                for s in range(phys)
            ]
            for t in range(phys):
                bank_ref[slot, t, :, c * COLS : (c + 1) * COLS] = sum(
                    look_ref[slot, s, t] * own[s] for s in range(phys)
                )


def pick_kernel(pair_ref, *refs):
    kept, outs = refs[:-2], refs[-2:]
    count = len(kept) // 2
    pair = pair_ref[:1, :1]
    for q in range(2):
        value = kept[q * count][...]
        for p in range(1, count):
            value = jnp.where(pair == p, kept[q * count + p][...], value)
        outs[q][...] = value


def second_kernel(moved_ref, tensor_ref, env_ref):
    gather(moved_ref, tensor_ref, env_ref)


def home_kernel(now, pair_ref, moved_ref, tensor_ref, even_ref, odd_ref, six_ref, out_ref, env):
    gather(moved_ref, tensor_ref, env)
    rows = env.shape[0]
    panel = rows // 2
    here = pair_ref[:1, :1] == now
    values = jnp.sum(moved_ref[:, rows:].astype(jnp.float32), axis=0)
    for q, (kept, last) in enumerate(((even_ref, six_ref), (odd_ref, env))):
        result = jnp.where(here, last[...], kept[...])
        value = values[:, q * 128 : (q + 1) * 128]
        extra = two_parts(value[:8] + value[8:])
        extra = jnp.concatenate([extra, jnp.zeros_like(extra)], axis=0)
        width = result.shape[1]
        for h in range(2):
            out_ref[2 * q + h, :, :width] = result[h * panel : (h + 1) * panel]
            out_ref[2 * q + h, :, width:] = extra


def out_kernel(home_ref, out_ref, value_ref):
    fronts, width = out_ref.shape[1], out_ref.shape[3]
    out_ref[0] = home_ref[:, :, :width]
    lane = lax.broadcasted_iota(jnp.int32, (1, 128), 1)
    values = jnp.zeros((1, 128), jnp.float32)
    for f in range(fronts):
        rows = home_ref[f, :, width:].astype(jnp.float32)
        value = jnp.sum(jnp.sum(rows, axis=0, keepdims=True), axis=1, keepdims=True)
        values = jnp.where(lane == f, value, values)
    value_ref[...] = values[:, :fronts]


def mix_kernel(
    width, where_ref, site_ref, kind_ref, operators_ref, probe_ref, mix_ref, look_ref, factor_ref, pair_ref
):
    pair, front = where_ref[1], where_ref[6]
    pair_ref[...] = jnp.zeros_like(pair_ref) + pair
    kind, site = kind_ref[front], site_ref[front]
    phys = probe_ref.shape[0]
    scale = 1.0 / math.sqrt(width)
    for slot in range(2):
        for s in range(phys):
            for t in range(phys):
                row, col = (s, t) if slot == 0 else (t, s)
                own = 1.0 if s == t else 0.0
                factor = jnp.where(site == 2 * pair + slot, operators_ref[kind, row, col], own)
                mix_ref[slot, s, t] = factor
                line = (slot * phys + s) * phys + t
                factor_ref[line : line + 1] = jnp.zeros((1, factor_ref.shape[1]), jnp.float32) + factor
                look_ref[slot, s, t] = probe_ref[row, col] * scale


def cut_kernel(
    where_ref, mine_ref, near_ref, start_ref, other_ref, keep_ref, give_ref, env_ref, sem
):
    core, half, front, parity = where_ref[4], where_ref[5], where_ref[6], where_ref[7]
    panel = other_ref.shape[0]
    copy = pltpu.make_async_copy(
        start_ref.at[front], env_ref.at[pl.ds(pl.multiple_of(half * panel, panel), panel)], sem.at[0]
    )
    copy.start()
    env_ref[pl.ds(pl.multiple_of((1 - half) * panel, panel), panel)] = other_ref[...]
    wide = keep_ref.shape[2]
    mine, near = mine_ref[...], near_ref[...]
    begun = jnp.where(parity == 0, mine, near)
    low, high = begun[..., :wide], begun[..., wide:]
    keep_ref[...] = jnp.where(core == 0, low, high)
    give_ref[...] = jnp.where(core == 0, high, low)
    copy.wait()


SMEM = pl.BlockSpec(memory_space=pltpu.SMEM)
VMEM = pl.BlockSpec(memory_space=pltpu.VMEM)
ANY = pl.BlockSpec(memory_space=pl.ANY)
HBM = pl.BlockSpec(memory_space=pltpu.HBM)


def params():
    return pltpu.CompilerParams(vmem_limit_bytes=16 * MIB)


def shifts(side, by, first):
    pairs = []
    for y in range(side):
        for x in range(side):
            for core in range(2):
                across = (core == 0) == first
                to = y * side + (x + by) % side if across else (y + by) % side * side + x
                pairs.append(((y * side + x) * 2 + core, to * 2 + core))
    return pairs


def in_hbm(arrays):
    return [pltpu.with_memory_space_constraint(a, pltpu.HBM) for a in arrays]


def first_ring(keep, give, core, side):
    bond = ("half", "member")
    other = lax.ppermute(give, bond, twins(side))
    chip = jnp.where(core == 0, jnp.stack([keep, other]), jnp.stack([other, keep]))
    return jnp.stack([chip] + [lax.ppermute(chip, bond, shifts(side, k, True)) for k in range(1, side)])


def second_ring(row, side):
    bond = ("half", "member")
    return [row] + [lax.ppermute(row, bond, shifts(side, m, False)) for m in range(1, side)]


def swap_cores(pieces, side):
    return [lax.ppermute(p, ("half", "member"), twins(side)) for p in pieces]


def twins(side):
    return [(i, i ^ 1) for i in range(2 * side * side)]


def on_device(site_tensors, start_env, operators, op_site, op_kind, probe):
    fronts, panel, width = start_env.shape
    phys = site_tensors.shape[2]
    kinds = operators.shape[0]
    pairs = lax.axis_size("pair")
    pair = lax.axis_index("pair")
    parity = lax.axis_index("parity")
    half = lax.axis_index("half")
    member = lax.axis_index("member")
    members = lax.axis_size("member")
    side = math.isqrt(members)
    rows = 2 * panel
    lanes = 2 * phys * panel
    f32 = jnp.float32
    bf16 = jnp.bfloat16
    core = member % 2
    chip = half * (members // 2) + member // 2
    front = 2 * parity + half
    where = jnp.stack([member, pair, chip // side, chip % side, core, half, front, parity]).astype(jnp.int32)

    mine = jnp.swapaxes(site_tensors[0], 0, 1)
    near = lax.ppermute(mine, "parity", [(0, 1), (1, 0)])
    given = lax.dynamic_index_in_dim(start_env, 2 * parity + 1 - half, 0, keepdims=False)
    other = lax.ppermute(given, "half", [(0, 1), (1, 0)])
    env_shape = jax.ShapeDtypeStruct((rows, width), bf16)
    square = jax.ShapeDtypeStruct((2, phys, phys), f32)
    part = jax.ShapeDtypeStruct((phys, panel, width // 2), bf16)
    bond = ("half", "member")
    mixes, looks, factors, pairs_here = pl.pallas_call(
        functools.partial(mix_kernel, width),
        in_specs=[SMEM] * 5,
        out_specs=[SMEM] * 2 + [VMEM] * 2,
        out_shape=[
            square,
            square,
            jax.ShapeDtypeStruct((2 * phys * phys, COLS), f32),
            jax.ShapeDtypeStruct((8, 128), jnp.int32),
        ],
        compiler_params=params(),
    )(where, op_site, op_kind, operators, probe)
    where, other, mine, near, mixes, looks, factors, pairs_here = lax.optimization_barrier(
        (where, other, mine, near, mixes, looks, factors, pairs_here)
    )
    small = (where, mixes, looks)
    after = lax.all_gather(jnp.where(parity == 0, near, mine), bond, axis=0)
    keep, give, env = pl.pallas_call(
        cut_kernel,
        in_specs=[SMEM] + [VMEM] * 2 + [ANY, VMEM],
        out_specs=[VMEM] * 3,
        out_shape=[part, part, env_shape],
        scratch_shapes=[pltpu.SemaphoreType.DMA((1,))],
        compiler_params=params(),
    )(where, mine, near, start_env, other)
    twin = lax.ppermute(env, bond, twins(side))
    row = first_ring(keep, give, core, side)
    row, twin = lax.optimization_barrier((row, twin))
    pieces = second_ring(row, side)
    swapped = swap_cores(pieces, side)

    def sent_shape(extra):
        return jax.ShapeDtypeStruct((members, rows + extra, lanes), bf16)

    seen_shape = jax.ShapeDtypeStruct((2, 8, 128), f32)

    def exchange(sent):
        return lax.all_to_all(sent, "member", 0, 0, tiled=True)

    sent, seen = pl.pallas_call(
        functools.partial(start_kernel, side),
        in_specs=[SMEM] * 3 + [VMEM] * 2 + [HBM] * side,
        out_specs=[VMEM] * 2,
        out_shape=[jax.ShapeDtypeStruct((members, panel, 2 * lanes), bf16), seen_shape],
        scratch_shapes=[
            pltpu.VMEM((side * side, 2, phys, panel, width // 2), bf16),
            pltpu.SemaphoreType.DMA((width // 2 // COLS, side, side)),
        ],
        compiler_params=params(),
    )(*small, env, twin, *in_hbm(pieces))
    moved = exchange(sent)
    whole = (side * side, 2, 2, phys, panel, width // 2)
    lay_sems = pltpu.SemaphoreType.DMA((2 * side, side))
    everything = pieces + swapped
    env = pl.pallas_call(
        functools.partial(pieces_kernel, side),
        in_specs=[SMEM, VMEM] + [HBM] * (2 * side),
        out_specs=VMEM,
        out_shape=env_shape,
        scratch_shapes=[pltpu.VMEM(whole, bf16), lay_sems],
        compiler_params=params(),
    )(where, moved, *in_hbm(everything))
    evens, odds = [env], []
    env, after = lax.optimization_barrier((env, after))
    sent, seen = pl.pallas_call(
        functools.partial(stream_kernel, 0),
        in_specs=[SMEM] * 3 + [VMEM, HBM, VMEM],
        out_specs=[VMEM] * 2,
        out_shape=[sent_shape(0), seen_shape],
        scratch_shapes=[
            pltpu.VMEM(after.shape, bf16),
            pltpu.SemaphoreType.DMA((width // COLS,)),
        ],
        compiler_params=params(),
    )(*small, env, *in_hbm([after]), seen)
    after = pltpu.with_memory_space_constraint(after, pltpu.VMEM)
    before = None
    for now in range(pairs - 1):
        if now > 0:
            sent, seen, env = pl.pallas_call(
                functools.partial(middle_kernel, now),
                in_specs=[VMEM] * 7,
                out_specs=[VMEM] * 3,
                out_shape=[sent_shape(0), seen_shape, env_shape],
                compiler_params=params(),
            )(*vectors, exchange(sent), before, after, seen)
            evens.append(env)
        env = pl.pallas_call(
            second_kernel,
            in_specs=[VMEM] * 2,
            out_specs=VMEM,
            out_shape=env_shape,
            compiler_params=params(),
        )(exchange(sent), after)
        odds.append(env)
        if now == 0:
            env, everything = lax.optimization_barrier((env, everything))
            before = pl.pallas_call(
                functools.partial(lay_kernel, side),
                in_specs=[SMEM] + [HBM] * (2 * side),
                out_specs=ANY,
                out_shape=jax.ShapeDtypeStruct(whole, bf16),
                scratch_shapes=[lay_sems],
                compiler_params=params(),
            )(where, *in_hbm(everything))
            before = pltpu.with_memory_space_constraint(before, pltpu.VMEM)
            bank = pl.pallas_call(
                bank_kernel,
                in_specs=[SMEM] * 2 + [VMEM] * 2,
                out_specs=VMEM,
                out_shape=jax.ShapeDtypeStruct((2, phys, rows, width), f32),
                compiler_params=params(),
            )(where, looks, before, after)
            vectors = (pairs_here, factors, bank)
        if now == pairs - 2:
            env, *kept = lax.optimization_barrier((env, *evens, *odds))
            picked = pl.pallas_call(
                pick_kernel,
                in_specs=[VMEM] * (1 + len(kept)),
                out_specs=[VMEM] * 2,
                out_shape=[env_shape] * 2,
                compiler_params=params(),
            )(pairs_here, *kept)
        env = lax.ppermute(env, "pair", [(now, now + 1)])
        if now == pairs - 2:
            env, picked = lax.optimization_barrier((env, picked))
        sent, seen = pl.pallas_call(
            functools.partial(first_kernel, now + 1),
            in_specs=[VMEM] * 6,
            out_specs=[VMEM] * 2,
            out_shape=[sent_shape(0), seen_shape],
            compiler_params=params(),
        )(*vectors, env, before, seen)
    moved = exchange(sent)
    sent, env = pl.pallas_call(
        functools.partial(end_kernel, pairs - 1),
        in_specs=[VMEM] * 7,
        out_specs=[VMEM] * 2,
        out_shape=[sent_shape(EXTRA), env_shape],
        compiler_params=params(),
    )(*vectors, moved, before, after, seen)
    homeward = pl.pallas_call(
        functools.partial(home_kernel, pairs - 1),
        in_specs=[VMEM] * 6,
        out_specs=VMEM,
        out_shape=jax.ShapeDtypeStruct((fronts, panel, width + 128), bf16),
        scratch_shapes=[pltpu.VMEM((rows, width), bf16)],
        compiler_params=params(),
    )(pairs_here, exchange(sent), after, *picked, env)
    home = lax.all_to_all(homeward, ("parity", "half"), 0, 0, tiled=True)
    out, values = pl.pallas_call(
        out_kernel,
        in_specs=[VMEM],
        out_specs=[VMEM] * 2,
        out_shape=[
            jax.ShapeDtypeStruct((1, fronts, panel, width), bf16),
            jax.ShapeDtypeStruct((1, fronts), f32),
        ],
        compiler_params=params(),
    )(home)
    return out, values.reshape(fronts, 1)


def solution(mesh):
    links, peers = mesh.devices.shape
    devices = mesh.devices.reshape(links // 2, 2, 2, peers // 2)
    chain, bond = ("pair", "parity"), ("half", "member")
    placed = (P(chain, bond, None, None), P(None, bond, None), P(), P(), P(), P())
    return jax.shard_map(
        on_device,
        mesh=Mesh(devices, chain + bond),
        in_specs=placed,
        out_specs=(P(chain, None, bond, None), P(None, chain)),
        check_vma=False,
    )
```

```python
import functools
import math

import jax
import jax.numpy as jnp
from jax import lax
from jax.experimental import pallas as pl
from jax.experimental.pallas import tpu as pltpu
from jax.sharding import Mesh
from jax.sharding import PartitionSpec as P

EXTRA = 16
MIB = 1 << 20
COLS = 256


def two_parts(value):
    high = value.astype(jnp.bfloat16).astype(jnp.float32)
    return jnp.concatenate([high, value - high], axis=0).astype(jnp.bfloat16)


def columns(tensor_ref, t, c):
    if len(tensor_ref.shape) == 4:
        return tensor_ref[:, t, :, c * COLS : (c + 1) * COLS].reshape(-1, COLS)
    per = tensor_ref.shape[5] // COLS
    at = c % per * COLS
    return tensor_ref[:, c // per, :, t, :, at : at + COLS].reshape(-1, COLS)


def block(tensor_ref, d, s, c):
    if len(tensor_ref.shape) == 4:
        return tensor_ref[d, s, :, c * COLS : (c + 1) * COLS].reshape(-1, COLS)
    per = tensor_ref.shape[5] // COLS
    at = c % per * COLS
    return tensor_ref[d // 2, c // per, d % 2, s, :, at : at + COLS].reshape(-1, COLS)


def spread(slot, where_ref, mix_ref, look_ref, env, tensor_ref, out_ref, arrived=None):
    width = env.shape[1]
    phys = mix_ref.shape[1]
    panel = env.shape[0] // 2
    half = width // panel // 2
    mem = where_ref[0]
    total = jnp.zeros((1, 128), jnp.float32)
    for c in range(width // COLS):
        if arrived is not None:
            arrived[c]()
        prods = [
            jnp.dot(env, columns(tensor_ref, t, c), preferred_element_type=jnp.float32)
            for t in range(phys)
        ]
        for s in range(phys):
            own = jnp.concatenate(
                [block(tensor_ref, h * half + mem, s, c) for h in range(2)], axis=0
            ).astype(jnp.float32)
            seen = own * sum(look_ref[slot, s, t] * prods[t] for t in range(phys))
            line = jnp.sum(seen, axis=0, keepdims=True)
            total += sum(line[:, b : b + 128] for b in range(0, COLS, 128))
        mixed = [sum(mix_ref[slot, s, t] * prods[t] for t in range(phys)) for s in range(phys)]
        tall = jnp.concatenate(
            [mixed[s][h * panel : (h + 1) * panel] for h in range(2) for s in range(phys)], axis=0
        )
        turned = tall.astype(jnp.bfloat16).T.reshape(COLS // panel, panel, 2 * phys * panel)
        first = c * (COLS // panel)
        h, first = first // half, first % half
        out_ref[first : first + COLS // panel, h * panel : (h + 1) * panel, :] = turned
    return total


def gather(moved_ref, tensor_ref, env_ref):
    rows, width = env_ref.shape
    half = moved_ref.shape[0]
    if moved_ref.shape[1] < rows:
        left = [
            jnp.concatenate([moved_ref[g], moved_ref[g + 1]], axis=0) for g in range(0, half, 2)
        ]
    else:
        left = [moved_ref[g, :rows] for g in range(half)]
    left = jnp.concatenate(left, axis=1)
    for c in range(width // COLS):
        right = jnp.concatenate(
            [
                block(tensor_ref, h * half + g, slice(None), c)
                for g in range(half)
                for h in range(2)
            ],
            axis=0,
        )
        env_ref[:, c * COLS : (c + 1) * COLS] = jnp.dot(
            left, right, preferred_element_type=jnp.float32
        ).astype(jnp.bfloat16)


def chip_of(side, where_ref, at, m, k):
    y, x = where_ref[2], where_ref[3]
    along = lax.rem(y + side - jnp.where(at == 0, m, k), side)
    across = lax.rem(x + side - jnp.where(at == 0, k, m), side)
    return along * side + across


def lay(side, where_ref, pieces, tensor_ref, sems):
    copies = []
    for i, ref in enumerate(pieces):
        at = where_ref[4] if i < side else 1 - where_ref[4]
        for k in range(side):
            place = tensor_ref.at[chip_of(side, where_ref, at, i % side, k), at]
            copies.append(pltpu.make_async_copy(ref.at[k], place, sems.at[i, k]))
    for copy in copies:
        copy.start()
    return copies


def lay_kernel(side, where_ref, *refs):
    for copy in lay(side, where_ref, refs[:-2], refs[-2], refs[-1]):
        copy.wait()


def pieces_kernel(side, where_ref, moved_ref, *refs):
    pieces, (env_ref, tensor, sems) = refs[:-3], refs[-3:]
    copies = lay(side, where_ref, pieces, tensor, sems)
    chips, wide = tensor.shape[0], tensor.shape[5]
    left = jnp.concatenate(
        [
            jnp.concatenate([moved_ref[g], moved_ref[g + 1]], axis=0) for g in range(0, chips, 2)
        ],
        axis=1,
    )
    for part in range(2):
        at = where_ref[4] if part == 0 else 1 - where_ref[4]
        for copy in copies[part * side * side : (part + 1) * side * side]:
            copy.wait()
        for c in range(wide // COLS):
            cols = slice(c * COLS, (c + 1) * COLS)
            right = jnp.concatenate(
                [
                    tensor[(h * chips + g) // 2, at, g % 2, :, :, cols].reshape(-1, COLS)
                    for g in range(chips)
                    for h in range(2)
                ],
                axis=0,
            )
            place = pl.ds(pl.multiple_of(at * wide + c * COLS, COLS), COLS)
            env_ref[:, place] = jnp.dot(
                left, right, preferred_element_type=jnp.float32
            ).astype(jnp.bfloat16)


def stream_kernel(
    now, where_ref, mix_ref, look_ref, env_ref, twin_ref, tensor_ref, seen_ref, out_ref, new_ref, held, sems
):
    core = where_ref[4]
    peers, phys, panel, wide = held.shape
    copies = []
    for c in range(wide // COLS):
        place = pl.ds(pl.multiple_of(core * wide + c * COLS, COLS), COLS)
        copies.append(
            pltpu.make_async_copy(
                tensor_ref.at[:, :, :, place], held.at[:, :, :, pl.ds(c * COLS, COLS)], sems.at[c]
            )
        )
        copies[-1].start()
    own, twin = env_ref[...], twin_ref[...]
    env = jnp.concatenate(
        [jnp.where(core == 0, own, twin), jnp.where(core == 0, twin, own)], axis=0
    )
    even = where_ref[0] - core
    total = jnp.zeros(new_ref.shape[1:], jnp.float32)
    for c, copy in enumerate(copies):
        copy.wait()
        cols = slice(c * COLS, (c + 1) * COLS)
        prods = [
            jnp.dot(env, held[:, t, :, cols].reshape(-1, COLS), preferred_element_type=jnp.float32)
            for t in range(phys)
        ]
        for s in range(phys):
            rows = [held[h * (peers // 2) + even + o, s, :, cols] for o in range(2) for h in range(2)]
            seen = jnp.concatenate(rows, axis=0).astype(jnp.float32)
            seen = seen * sum(look_ref[1, s, t] * prods[t] for t in range(phys))
            seen = jnp.sum(seen.reshape(-1, 8, COLS), axis=0)
            total += sum(seen[:, b : b + 128] for b in range(0, COLS, 128))
        mixed = [sum(mix_ref[1, s, t] * prods[t] for t in range(phys)) for s in range(phys)]
        tall = [mixed[s][q * panel : (q + 1) * panel] for q in range(4) for s in range(phys)]
        turned = jnp.concatenate(tall, axis=0).astype(jnp.bfloat16).T
        per = COLS // panel
        out_ref[c * per : (c + 1) * per] = turned.reshape(per, panel, 4 * phys * panel)
    new_ref[0] = seen_ref[0]
    new_ref[1] = total


def load(side, where_ref, pieces, tensor_ref, sems):
    blocks = []
    for c in range(tensor_ref.shape[4] // COLS):
        cols = pl.ds(c * COLS, COLS)
        copies = []
        for m, ref in enumerate(pieces):
            for k in range(side):
                chip = chip_of(side, where_ref, where_ref[4], m, k)
                copies.append(
                    pltpu.make_async_copy(
                        ref.at[k, :, :, :, cols], tensor_ref.at[chip, :, :, :, cols], sems.at[c, m, k]
                    )
                )
        for copy in copies:
            copy.start()
        blocks.append(copies)
    return blocks


def start_kernel(side, where_ref, mix_ref, look_ref, env_ref, twin_ref, *refs):
    pieces, (out_ref, new_ref, tensor, sems) = refs[:-4], refs[-4:]
    core = where_ref[4]
    blocks = load(side, where_ref, pieces, tensor, sems)
    own, twin = env_ref[...], twin_ref[...]
    env = jnp.concatenate(
        [jnp.where(core == 0, own, twin), jnp.where(core == 0, twin, own)], axis=0
    )
    chips, _, phys, panel, wide = tensor.shape
    mem = where_ref[0] // 2
    total = jnp.zeros((1, 128), jnp.float32)
    for c, copies in enumerate(blocks):
        for copy in copies:
            copy.wait()
        cols = slice(c * COLS, (c + 1) * COLS)
        prods = [
            jnp.dot(
                env, tensor[:, :, t, :, cols].reshape(-1, COLS), preferred_element_type=jnp.float32
            )
            for t in range(phys)
        ]
        for s in range(phys):
            rows = [tensor[h * (chips // 2) + mem, o, s, :, cols] for o in range(2) for h in range(2)]
            seen = jnp.concatenate(rows, axis=0).astype(jnp.float32)
            seen = seen * sum(look_ref[0, s, t] * prods[t] for t in range(phys))
            line = jnp.sum(seen, axis=0, keepdims=True)
            total += sum(line[:, b : b + 128] for b in range(0, COLS, 128))
        mixed = [sum(mix_ref[0, s, t] * prods[t] for t in range(phys)) for s in range(phys)]
        tall = [mixed[s][q * panel : (q + 1) * panel] for q in range(4) for s in range(phys)]
        turned = jnp.concatenate(tall, axis=0).astype(jnp.bfloat16).T
        per = COLS // panel
        out_ref[c * per : (c + 1) * per] = turned.reshape(per, panel, 4 * phys * panel)
    first_row = lax.broadcasted_iota(jnp.int32, new_ref.shape[1:], 0) == 0
    total = jnp.where(first_row, jnp.broadcast_to(total, new_ref.shape[1:]), 0.0)
    new_ref[...] = jnp.broadcast_to(total[None], new_ref.shape)


def spread_plain(slot, mix_ref, bank_ref, env, tensor_ref, out_ref):
    width = env.shape[1]
    phys = bank_ref.shape[1]
    panel = env.shape[0] // 2
    half = width // panel // 2
    total = jnp.zeros((8, 128), jnp.float32)
    for c in range(width // COLS):
        prods = [
            jnp.dot(env, columns(tensor_ref, t, c), preferred_element_type=jnp.float32)
            for t in range(phys)
        ]
        seen = sum(bank_ref[slot, t, :, c * COLS : (c + 1) * COLS] * prods[t] for t in range(phys))
        seen = jnp.sum(seen.reshape(-1, 8, COLS), axis=0)
        total += sum(seen[:, b : b + 128] for b in range(0, COLS, 128))

        def factor(s, t):
            row = slot * phys * phys + s * phys + t
            return mix_ref[row : row + 1]

        mixed = [sum(factor(s, t) * prods[t] for t in range(phys)) for s in range(phys)]
        tall = jnp.concatenate(
            [mixed[s][h * panel : (h + 1) * panel] for h in range(2) for s in range(phys)], axis=0
        )
        turned = tall.astype(jnp.bfloat16).T.reshape(COLS // panel, panel, 2 * phys * panel)
        first = c * (COLS // panel)
        h, first = first // half, first % half
        out_ref[first : first + COLS // panel, h * panel : (h + 1) * panel, :] = turned
    return total


def first_kernel(now, pair_ref, mix_ref, bank_ref, env_ref, tensor_ref, seen_ref, out_ref, new_ref):
    total = spread_plain(0, mix_ref, bank_ref, env_ref[...], tensor_ref, out_ref)
    new_ref[0] = jnp.where(pair_ref[...] == now, total, seen_ref[0])
    new_ref[1] = seen_ref[1]


def middle_kernel(
    now, pair_ref, mix_ref, bank_ref, moved_ref, old_ref, tensor_ref, seen_ref, out_ref, new_ref, env_ref
):
    gather(moved_ref, old_ref, env_ref)
    total = spread_plain(1, mix_ref, bank_ref, env_ref[...], tensor_ref, out_ref)
    new_ref[0] = seen_ref[0]
    new_ref[1] = jnp.where(pair_ref[...] == now, total, seen_ref[1])


def end_kernel(
    now, pair_ref, mix_ref, bank_ref, moved_ref, old_ref, tensor_ref, seen_ref, out_ref, env_ref
):
    gather(moved_ref, old_ref, env_ref)
    total = spread_plain(1, mix_ref, bank_ref, env_ref[...], tensor_ref, out_ref)
    rows, lanes = env_ref.shape[0], out_ref.shape[2]
    odd = jnp.where(pair_ref[...] == now, total, seen_ref[1])
    extra = jnp.concatenate([two_parts(v) for v in (seen_ref[0], odd)], axis=1)
    out_ref[:, rows:, :] = jnp.broadcast_to(extra[None], (out_ref.shape[0], EXTRA, lanes))


def bank_kernel(where_ref, look_ref, *refs):
    tensors, bank_ref = refs[:-1], refs[-1]
    slots, phys, rows, width = bank_ref.shape
    half = width // rows
    for slot, ref in enumerate(tensors):
        for c in range(width // COLS):
            own = [
                jnp.concatenate(
                    [block(ref, h * half + where_ref[0], s, c) for h in range(2)], axis=0
                ).astype(jnp.float32)
                for s in range(phys)
            ]
            for t in range(phys):
                bank_ref[slot, t, :, c * COLS : (c + 1) * COLS] = sum(
                    look_ref[slot, s, t] * own[s] for s in range(phys)
                )


def pick_kernel(pair_ref, *refs):
    kept, outs = refs[:-2], refs[-2:]
    count = len(kept) // 2
    pair = pair_ref[:1, :1]
    for q in range(2):
        value = kept[q * count][...]
        for p in range(1, count):
            value = jnp.where(pair == p, kept[q * count + p][...], value)
        outs[q][...] = value


def second_kernel(moved_ref, tensor_ref, env_ref):
    gather(moved_ref, tensor_ref, env_ref)


def home_kernel(now, pair_ref, moved_ref, tensor_ref, even_ref, odd_ref, six_ref, out_ref, env):
    gather(moved_ref, tensor_ref, env)
    rows = env.shape[0]
    panel = rows // 2
    here = pair_ref[:1, :1] == now
    values = jnp.sum(moved_ref[:, rows:].astype(jnp.float32), axis=0)
    for q, (kept, last) in enumerate(((even_ref, six_ref), (odd_ref, env))):
        result = jnp.where(here, last[...], kept[...])
        value = values[:, q * 128 : (q + 1) * 128]
        extra = two_parts(value[:8] + value[8:])
        extra = jnp.concatenate([extra, jnp.zeros_like(extra)], axis=0)
        width = result.shape[1]
        for h in range(2):
            out_ref[2 * q + h, :, :width] = result[h * panel : (h + 1) * panel]
            out_ref[2 * q + h, :, width:] = extra


def out_kernel(home_ref, out_ref, value_ref):
    fronts, width = out_ref.shape[1], out_ref.shape[3]
    out_ref[0] = home_ref[:, :, :width]
    lane = lax.broadcasted_iota(jnp.int32, (1, 128), 1)
    values = jnp.zeros((1, 128), jnp.float32)
    for f in range(fronts):
        rows = home_ref[f, :, width:].astype(jnp.float32)
        value = jnp.sum(jnp.sum(rows, axis=0, keepdims=True), axis=1, keepdims=True)
        values = jnp.where(lane == f, value, values)
    value_ref[...] = values[:, :fronts]


def mix_kernel(
    width, where_ref, site_ref, kind_ref, operators_ref, probe_ref, mix_ref, look_ref, factor_ref, pair_ref
):
    pair, front = where_ref[1], where_ref[6]
    pair_ref[...] = jnp.zeros_like(pair_ref) + pair
    kind, site = kind_ref[front], site_ref[front]
    phys = probe_ref.shape[0]
    scale = 1.0 / math.sqrt(width)
    for slot in range(2):
        for s in range(phys):
            for t in range(phys):
                row, col = (s, t) if slot == 0 else (t, s)
                own = 1.0 if s == t else 0.0
                factor = jnp.where(site == 2 * pair + slot, operators_ref[kind, row, col], own)
                mix_ref[slot, s, t] = factor
                line = (slot * phys + s) * phys + t
                factor_ref[line : line + 1] = jnp.zeros((1, factor_ref.shape[1]), jnp.float32) + factor
                look_ref[slot, s, t] = probe_ref[row, col] * scale


def cut_kernel(
    where_ref, mine_ref, near_ref, start_ref, other_ref, keep_ref, give_ref, env_ref, sem
):
    core, half, front, parity = where_ref[4], where_ref[5], where_ref[6], where_ref[7]
    panel = other_ref.shape[0]
    copy = pltpu.make_async_copy(
        start_ref.at[front], env_ref.at[pl.ds(pl.multiple_of(half * panel, panel), panel)], sem.at[0]
    )
    copy.start()
    env_ref[pl.ds(pl.multiple_of((1 - half) * panel, panel), panel)] = other_ref[...]
    wide = keep_ref.shape[2]
    mine, near = mine_ref[...], near_ref[...]
    begun = jnp.where(parity == 0, mine, near)
    low, high = begun[..., :wide], begun[..., wide:]
    keep_ref[...] = jnp.where(core == 0, low, high)
    give_ref[...] = jnp.where(core == 0, high, low)
    copy.wait()


SMEM = pl.BlockSpec(memory_space=pltpu.SMEM)
VMEM = pl.BlockSpec(memory_space=pltpu.VMEM)
ANY = pl.BlockSpec(memory_space=pl.ANY)
HBM = pl.BlockSpec(memory_space=pltpu.HBM)


def params():
    return pltpu.CompilerParams(vmem_limit_bytes=16 * MIB)


def shifts(side, by, first):
    pairs = []
    for y in range(side):
        for x in range(side):
            for core in range(2):
                across = (core == 0) == first
                to = y * side + (x + by) % side if across else (y + by) % side * side + x
                pairs.append(((y * side + x) * 2 + core, to * 2 + core))
    return pairs


def in_hbm(arrays):
    return [pltpu.with_memory_space_constraint(a, pltpu.HBM) for a in arrays]


def first_ring(keep, give, core, side):
    bond = ("half", "member")
    other = lax.ppermute(give, bond, twins(side))
    chip = jnp.where(core == 0, jnp.stack([keep, other]), jnp.stack([other, keep]))
    return jnp.stack([chip] + [lax.ppermute(chip, bond, shifts(side, k, True)) for k in range(1, side)])


def second_ring(row, side):
    bond = ("half", "member")
    return [row] + [lax.ppermute(row, bond, shifts(side, m, False)) for m in range(1, side)]


def swap_cores(pieces, side):
    return [lax.ppermute(p, ("half", "member"), twins(side)) for p in pieces]


def twins(side):
    return [(i, i ^ 1) for i in range(2 * side * side)]


def on_device(site_tensors, start_env, operators, op_site, op_kind, probe):
    fronts, panel, width = start_env.shape
    phys = site_tensors.shape[2]
    kinds = operators.shape[0]
    pairs = lax.axis_size("pair")
    pair = lax.axis_index("pair")
    parity = lax.axis_index("parity")
    half = lax.axis_index("half")
    member = lax.axis_index("member")
    members = lax.axis_size("member")
    side = math.isqrt(members)
    rows = 2 * panel
    lanes = 2 * phys * panel
    f32 = jnp.float32
    bf16 = jnp.bfloat16
    core = member % 2
    chip = half * (members // 2) + member // 2
    front = 2 * parity + half
    where = jnp.stack([member, pair, chip // side, chip % side, core, half, front, parity]).astype(jnp.int32)

    mine = jnp.swapaxes(site_tensors[0], 0, 1)
    near = lax.ppermute(mine, "parity", [(0, 1), (1, 0)])
    given = lax.dynamic_index_in_dim(start_env, 2 * parity + 1 - half, 0, keepdims=False)
    other = lax.ppermute(given, "half", [(0, 1), (1, 0)])
    env_shape = jax.ShapeDtypeStruct((rows, width), bf16)
    square = jax.ShapeDtypeStruct((2, phys, phys), f32)
    part = jax.ShapeDtypeStruct((phys, panel, width // 2), bf16)
    bond = ("half", "member")
    mixes, looks, factors, pairs_here = pl.pallas_call(
        functools.partial(mix_kernel, width),
        in_specs=[SMEM] * 5,
        out_specs=[SMEM] * 2 + [VMEM] * 2,
        out_shape=[
            square,
            square,
            jax.ShapeDtypeStruct((2 * phys * phys, COLS), f32),
            jax.ShapeDtypeStruct((8, 128), jnp.int32),
        ],
        compiler_params=params(),
    )(where, op_site, op_kind, operators, probe)
    where, other, mine, near, mixes, looks, factors, pairs_here = lax.optimization_barrier(
        (where, other, mine, near, mixes, looks, factors, pairs_here)
    )
    small = (where, mixes, looks)
    after = lax.all_gather(jnp.where(parity == 0, near, mine), bond, axis=0)
    keep, give, env = pl.pallas_call(
        cut_kernel,
        in_specs=[SMEM] + [VMEM] * 2 + [ANY, VMEM],
        out_specs=[VMEM] * 3,
        out_shape=[part, part, env_shape],
        scratch_shapes=[pltpu.SemaphoreType.DMA((1,))],
        compiler_params=params(),
    )(where, mine, near, start_env, other)
    twin = lax.ppermute(env, bond, twins(side))
    row = first_ring(keep, give, core, side)
    row, twin = lax.optimization_barrier((row, twin))
    pieces = second_ring(row, side)
    swapped = swap_cores(pieces, side)

    def sent_shape(extra):
        return jax.ShapeDtypeStruct((members, rows + extra, lanes), bf16)

    seen_shape = jax.ShapeDtypeStruct((2, 8, 128), f32)

    def exchange(sent):
        return lax.all_to_all(sent, "member", 0, 0, tiled=True)

    sent, seen = pl.pallas_call(
        functools.partial(start_kernel, side),
        in_specs=[SMEM] * 3 + [VMEM] * 2 + [HBM] * side,
        out_specs=[VMEM] * 2,
        out_shape=[jax.ShapeDtypeStruct((members, panel, 2 * lanes), bf16), seen_shape],
        scratch_shapes=[
            pltpu.VMEM((side * side, 2, phys, panel, width // 2), bf16),
            pltpu.SemaphoreType.DMA((width // 2 // COLS, side, side)),
        ],
        compiler_params=params(),
    )(*small, env, twin, *in_hbm(pieces))
    moved = exchange(sent)
    whole = (side * side, 2, 2, phys, panel, width // 2)
    lay_sems = pltpu.SemaphoreType.DMA((2 * side, side))
    everything = pieces + swapped
    env = pl.pallas_call(
        functools.partial(pieces_kernel, side),
        in_specs=[SMEM, VMEM] + [HBM] * (2 * side),
        out_specs=VMEM,
        out_shape=env_shape,
        scratch_shapes=[pltpu.VMEM(whole, bf16), lay_sems],
        compiler_params=params(),
    )(where, moved, *in_hbm(everything))
    evens, odds = [env], []
    twin = lax.ppermute(env, bond, twins(side))
    env, twin, after = lax.optimization_barrier((env, twin, after))
    sent, seen = pl.pallas_call(
        functools.partial(stream_kernel, 0),
        in_specs=[SMEM] * 3 + [VMEM] * 2 + [HBM, VMEM],
        out_specs=[VMEM] * 2,
        out_shape=[jax.ShapeDtypeStruct((members, panel, 2 * lanes), bf16), seen_shape],
        scratch_shapes=[
            pltpu.VMEM(after.shape[:3] + (width // 2,), bf16),
            pltpu.SemaphoreType.DMA((width // 2 // COLS,)),
        ],
        compiler_params=params(),
    )(*small, env, twin, *in_hbm([after]), seen)
    after = pltpu.with_memory_space_constraint(after, pltpu.VMEM)
    before = None
    for now in range(pairs - 1):
        if now > 0:
            sent, seen, env = pl.pallas_call(
                functools.partial(middle_kernel, now),
                in_specs=[VMEM] * 7,
                out_specs=[VMEM] * 3,
                out_shape=[sent_shape(0), seen_shape, env_shape],
                compiler_params=params(),
            )(*vectors, exchange(sent), before, after, seen)
            evens.append(env)
        env = pl.pallas_call(
            second_kernel,
            in_specs=[VMEM] * 2,
            out_specs=VMEM,
            out_shape=env_shape,
            compiler_params=params(),
        )(exchange(sent), after)
        odds.append(env)
        if now == 0:
            env, everything = lax.optimization_barrier((env, everything))
            before = pl.pallas_call(
                functools.partial(lay_kernel, side),
                in_specs=[SMEM] + [HBM] * (2 * side),
                out_specs=ANY,
                out_shape=jax.ShapeDtypeStruct(whole, bf16),
                scratch_shapes=[lay_sems],
                compiler_params=params(),
            )(where, *in_hbm(everything))
            before = pltpu.with_memory_space_constraint(before, pltpu.VMEM)
            bank = pl.pallas_call(
                bank_kernel,
                in_specs=[SMEM] * 2 + [VMEM] * 2,
                out_specs=VMEM,
                out_shape=jax.ShapeDtypeStruct((2, phys, rows, width), f32),
                compiler_params=params(),
            )(where, looks, before, after)
            vectors = (pairs_here, factors, bank)
        if now == pairs - 2:
            env, *kept = lax.optimization_barrier((env, *evens, *odds))
            picked = pl.pallas_call(
                pick_kernel,
                in_specs=[VMEM] * (1 + len(kept)),
                out_specs=[VMEM] * 2,
                out_shape=[env_shape] * 2,
                compiler_params=params(),
            )(pairs_here, *kept)
        env = lax.ppermute(env, "pair", [(now, now + 1)])
        if now == pairs - 2:
            env, picked = lax.optimization_barrier((env, picked))
        sent, seen = pl.pallas_call(
            functools.partial(first_kernel, now + 1),
            in_specs=[VMEM] * 6,
            out_specs=[VMEM] * 2,
            out_shape=[sent_shape(0), seen_shape],
            compiler_params=params(),
        )(*vectors, env, before, seen)
    moved = exchange(sent)
    sent, env = pl.pallas_call(
        functools.partial(end_kernel, pairs - 1),
        in_specs=[VMEM] * 7,
        out_specs=[VMEM] * 2,
        out_shape=[sent_shape(EXTRA), env_shape],
        compiler_params=params(),
    )(*vectors, moved, before, after, seen)
    homeward = pl.pallas_call(
        functools.partial(home_kernel, pairs - 1),
        in_specs=[VMEM] * 6,
        out_specs=VMEM,
        out_shape=jax.ShapeDtypeStruct((fronts, panel, width + 128), bf16),
        scratch_shapes=[pltpu.VMEM((rows, width), bf16)],
        compiler_params=params(),
    )(pairs_here, exchange(sent), after, *picked, env)
    home = lax.all_to_all(homeward, ("parity", "half"), 0, 0, tiled=True)
    out, values = pl.pallas_call(
        out_kernel,
        in_specs=[VMEM],
        out_specs=[VMEM] * 2,
        out_shape=[
            jax.ShapeDtypeStruct((1, fronts, panel, width), bf16),
            jax.ShapeDtypeStruct((1, fronts), f32),
        ],
        compiler_params=params(),
    )(home)
    return out, values.reshape(fronts, 1)


def solution(mesh):
    links, peers = mesh.devices.shape
    devices = mesh.devices.reshape(links // 2, 2, 2, peers // 2)
    chain, bond = ("pair", "parity"), ("half", "member")
    placed = (P(chain, bond, None, None), P(None, bond, None), P(), P(), P(), P())
    return jax.shard_map(
        on_device,
        mesh=Mesh(devices, chain + bond),
        in_specs=placed,
        out_specs=(P(chain, None, bond, None), P(None, chain)),
        check_vma=False,
    )
```

```python
import functools
import math

import jax
import jax.numpy as jnp
from jax import lax
from jax.experimental import pallas as pl
from jax.experimental.pallas import tpu as pltpu
from jax.sharding import Mesh
from jax.sharding import PartitionSpec as P

EXTRA = 16
MIB = 1 << 20
COLS = 256


def two_parts(value):
    high = value.astype(jnp.bfloat16).astype(jnp.float32)
    return jnp.concatenate([high, value - high], axis=0).astype(jnp.bfloat16)


def for_first_pair(kernel):
    def guarded(static, where_ref, *refs):
        pl.when(where_ref[1] == 0)(functools.partial(kernel, static, where_ref, *refs))

    return guarded


def columns(tensor_ref, t, c):
    if len(tensor_ref.shape) == 4:
        return tensor_ref[:, t, :, c * COLS : (c + 1) * COLS].reshape(-1, COLS)
    per = tensor_ref.shape[5] // COLS
    at = c % per * COLS
    return tensor_ref[:, c // per, :, t, :, at : at + COLS].reshape(-1, COLS)


def block(tensor_ref, d, s, c):
    if len(tensor_ref.shape) == 4:
        return tensor_ref[d, s, :, c * COLS : (c + 1) * COLS].reshape(-1, COLS)
    per = tensor_ref.shape[5] // COLS
    at = c % per * COLS
    return tensor_ref[d // 2, c // per, d % 2, s, :, at : at + COLS].reshape(-1, COLS)


def spread(slot, where_ref, mix_ref, look_ref, env, tensor_ref, out_ref, arrived=None):
    width = env.shape[1]
    phys = mix_ref.shape[1]
    panel = env.shape[0] // 2
    half = width // panel // 2
    mem = where_ref[0]
    total = jnp.zeros((1, 128), jnp.float32)
    for c in range(width // COLS):
        if arrived is not None:
            arrived[c]()
        prods = [
            jnp.dot(env, columns(tensor_ref, t, c), preferred_element_type=jnp.float32)
            for t in range(phys)
        ]
        for s in range(phys):
            own = jnp.concatenate(
                [block(tensor_ref, h * half + mem, s, c) for h in range(2)], axis=0
            ).astype(jnp.float32)
            seen = own * sum(look_ref[slot, s, t] * prods[t] for t in range(phys))
            line = jnp.sum(seen, axis=0, keepdims=True)
            total += sum(line[:, b : b + 128] for b in range(0, COLS, 128))
        mixed = [sum(mix_ref[slot, s, t] * prods[t] for t in range(phys)) for s in range(phys)]
        tall = jnp.concatenate(
            [mixed[s][h * panel : (h + 1) * panel] for h in range(2) for s in range(phys)], axis=0
        )
        turned = tall.astype(jnp.bfloat16).T.reshape(COLS // panel, panel, 2 * phys * panel)
        first = c * (COLS // panel)
        h, first = first // half, first % half
        out_ref[first : first + COLS // panel, h * panel : (h + 1) * panel, :] = turned
    return total


def gather(moved_ref, tensor_ref, env_ref):
    rows, width = env_ref.shape
    half = moved_ref.shape[0]
    if moved_ref.shape[1] < rows:
        left = [
            jnp.concatenate([moved_ref[g], moved_ref[g + 1]], axis=0) for g in range(0, half, 2)
        ]
    else:
        left = [moved_ref[g, :rows] for g in range(half)]
    left = jnp.concatenate(left, axis=1)
    for c in range(width // COLS):
        right = jnp.concatenate(
            [
                block(tensor_ref, h * half + g, slice(None), c)
                for g in range(half)
                for h in range(2)
            ],
            axis=0,
        )
        env_ref[:, c * COLS : (c + 1) * COLS] = jnp.dot(
            left, right, preferred_element_type=jnp.float32
        ).astype(jnp.bfloat16)


def chip_of(side, where_ref, at, m, k):
    y, x = where_ref[2], where_ref[3]
    along = lax.rem(y + side - jnp.where(at == 0, m, k), side)
    across = lax.rem(x + side - jnp.where(at == 0, k, m), side)
    return along * side + across


def lay(side, where_ref, pieces, tensor_ref, sems):
    copies = []
    for i, ref in enumerate(pieces):
        at = where_ref[4] if i < side else 1 - where_ref[4]
        for k in range(side):
            place = tensor_ref.at[chip_of(side, where_ref, at, i % side, k), at]
            copies.append(pltpu.make_async_copy(ref.at[k], place, sems.at[i, k]))
    for copy in copies:
        copy.start()
    return copies


def lay_kernel(side, where_ref, *refs):
    for copy in lay(side, where_ref, refs[:-2], refs[-2], refs[-1]):
        copy.wait()


@for_first_pair
def pieces_kernel(side, where_ref, moved_ref, *refs):
    pieces, (env_ref, tensor, sems) = refs[:-3], refs[-3:]
    copies = lay(side, where_ref, pieces, tensor, sems)
    chips, wide = tensor.shape[0], tensor.shape[5]
    left = jnp.concatenate(
        [
            jnp.concatenate([moved_ref[g], moved_ref[g + 1]], axis=0) for g in range(0, chips, 2)
        ],
        axis=1,
    )
    for part in range(2):
        at = where_ref[4] if part == 0 else 1 - where_ref[4]
        for copy in copies[part * side * side : (part + 1) * side * side]:
            copy.wait()
        for c in range(wide // COLS):
            cols = slice(c * COLS, (c + 1) * COLS)
            right = jnp.concatenate(
                [
                    tensor[(h * chips + g) // 2, at, g % 2, :, :, cols].reshape(-1, COLS)
                    for g in range(chips)
                    for h in range(2)
                ],
                axis=0,
            )
            place = pl.ds(pl.multiple_of(at * wide + c * COLS, COLS), COLS)
            env_ref[:, place] = jnp.dot(
                left, right, preferred_element_type=jnp.float32
            ).astype(jnp.bfloat16)


@for_first_pair
def stream_kernel(
    now, where_ref, mix_ref, look_ref, env_ref, twin_ref, tensor_ref, seen_ref, out_ref, new_ref, held, sems
):
    core = where_ref[4]
    peers, phys, panel, wide = held.shape
    copies = []
    for c in range(wide // COLS):
        place = pl.ds(pl.multiple_of(core * wide + c * COLS, COLS), COLS)
        copies.append(
            pltpu.make_async_copy(
                tensor_ref.at[:, :, :, place], held.at[:, :, :, pl.ds(c * COLS, COLS)], sems.at[c]
            )
        )
        copies[-1].start()
    own, twin = env_ref[...], twin_ref[...]
    env = jnp.concatenate(
        [jnp.where(core == 0, own, twin), jnp.where(core == 0, twin, own)], axis=0
    )
    even = where_ref[0] - core
    total = jnp.zeros(new_ref.shape[1:], jnp.float32)
    for c, copy in enumerate(copies):
        copy.wait()
        cols = slice(c * COLS, (c + 1) * COLS)
        prods = [
            jnp.dot(env, held[:, t, :, cols].reshape(-1, COLS), preferred_element_type=jnp.float32)
            for t in range(phys)
        ]
        for s in range(phys):
            rows = [held[h * (peers // 2) + even + o, s, :, cols] for o in range(2) for h in range(2)]
            seen = jnp.concatenate(rows, axis=0).astype(jnp.float32)
            seen = seen * sum(look_ref[1, s, t] * prods[t] for t in range(phys))
            seen = jnp.sum(seen.reshape(-1, 8, COLS), axis=0)
            total += sum(seen[:, b : b + 128] for b in range(0, COLS, 128))
        mixed = [sum(mix_ref[1, s, t] * prods[t] for t in range(phys)) for s in range(phys)]
        tall = [mixed[s][q * panel : (q + 1) * panel] for q in range(4) for s in range(phys)]
        turned = jnp.concatenate(tall, axis=0).astype(jnp.bfloat16).T
        per = COLS // panel
        out_ref[c * per : (c + 1) * per] = turned.reshape(per, panel, 4 * phys * panel)
    new_ref[0] = seen_ref[0]
    new_ref[1] = total


def load(side, where_ref, pieces, tensor_ref, sems):
    blocks = []
    for c in range(tensor_ref.shape[4] // COLS):
        cols = pl.ds(c * COLS, COLS)
        copies = []
        for m, ref in enumerate(pieces):
            for k in range(side):
                chip = chip_of(side, where_ref, where_ref[4], m, k)
                copies.append(
                    pltpu.make_async_copy(
                        ref.at[k, :, :, :, cols], tensor_ref.at[chip, :, :, :, cols], sems.at[c, m, k]
                    )
                )
        for copy in copies:
            copy.start()
        blocks.append(copies)
    return blocks


@for_first_pair
def start_kernel(side, where_ref, mix_ref, look_ref, env_ref, twin_ref, *refs):
    pieces, (out_ref, new_ref, tensor, sems) = refs[:-4], refs[-4:]
    core = where_ref[4]
    blocks = load(side, where_ref, pieces, tensor, sems)
    own, twin = env_ref[...], twin_ref[...]
    env = jnp.concatenate(
        [jnp.where(core == 0, own, twin), jnp.where(core == 0, twin, own)], axis=0
    )
    chips, _, phys, panel, wide = tensor.shape
    mem = where_ref[0] // 2
    total = jnp.zeros((1, 128), jnp.float32)
    for c, copies in enumerate(blocks):
        for copy in copies:
            copy.wait()
        cols = slice(c * COLS, (c + 1) * COLS)
        prods = [
            jnp.dot(
                env, tensor[:, :, t, :, cols].reshape(-1, COLS), preferred_element_type=jnp.float32
            )
            for t in range(phys)
        ]
        for s in range(phys):
            rows = [tensor[h * (chips // 2) + mem, o, s, :, cols] for o in range(2) for h in range(2)]
            seen = jnp.concatenate(rows, axis=0).astype(jnp.float32)
            seen = seen * sum(look_ref[0, s, t] * prods[t] for t in range(phys))
            line = jnp.sum(seen, axis=0, keepdims=True)
            total += sum(line[:, b : b + 128] for b in range(0, COLS, 128))
        mixed = [sum(mix_ref[0, s, t] * prods[t] for t in range(phys)) for s in range(phys)]
        tall = [mixed[s][q * panel : (q + 1) * panel] for q in range(4) for s in range(phys)]
        turned = jnp.concatenate(tall, axis=0).astype(jnp.bfloat16).T
        per = COLS // panel
        out_ref[c * per : (c + 1) * per] = turned.reshape(per, panel, 4 * phys * panel)
    first_row = lax.broadcasted_iota(jnp.int32, new_ref.shape[1:], 0) == 0
    total = jnp.where(first_row, jnp.broadcast_to(total, new_ref.shape[1:]), 0.0)
    new_ref[...] = jnp.broadcast_to(total[None], new_ref.shape)


def spread_plain(slot, mix_ref, bank_ref, env, tensor_ref, out_ref):
    width = env.shape[1]
    phys = bank_ref.shape[1]
    panel = env.shape[0] // 2
    half = width // panel // 2
    total = jnp.zeros((8, 128), jnp.float32)
    for c in range(width // COLS):
        prods = [
            jnp.dot(env, columns(tensor_ref, t, c), preferred_element_type=jnp.float32)
            for t in range(phys)
        ]
        seen = sum(bank_ref[slot, t, :, c * COLS : (c + 1) * COLS] * prods[t] for t in range(phys))
        seen = jnp.sum(seen.reshape(-1, 8, COLS), axis=0)
        total += sum(seen[:, b : b + 128] for b in range(0, COLS, 128))

        def factor(s, t):
            row = slot * phys * phys + s * phys + t
            return mix_ref[row : row + 1]

        mixed = [sum(factor(s, t) * prods[t] for t in range(phys)) for s in range(phys)]
        tall = jnp.concatenate(
            [mixed[s][h * panel : (h + 1) * panel] for h in range(2) for s in range(phys)], axis=0
        )
        turned = tall.astype(jnp.bfloat16).T.reshape(COLS // panel, panel, 2 * phys * panel)
        first = c * (COLS // panel)
        h, first = first // half, first % half
        out_ref[first : first + COLS // panel, h * panel : (h + 1) * panel, :] = turned
    return total


def first_kernel(now, pair_ref, mix_ref, bank_ref, env_ref, tensor_ref, seen_ref, out_ref, new_ref):
    total = spread_plain(0, mix_ref, bank_ref, env_ref[...], tensor_ref, out_ref)
    new_ref[0] = jnp.where(pair_ref[...] == now, total, seen_ref[0])
    new_ref[1] = seen_ref[1]


def middle_kernel(
    now, pair_ref, mix_ref, bank_ref, moved_ref, old_ref, tensor_ref, seen_ref, out_ref, new_ref, env_ref
):
    gather(moved_ref, old_ref, env_ref)
    total = spread_plain(1, mix_ref, bank_ref, env_ref[...], tensor_ref, out_ref)
    new_ref[0] = seen_ref[0]
    new_ref[1] = jnp.where(pair_ref[...] == now, total, seen_ref[1])


def end_kernel(
    now, pair_ref, mix_ref, bank_ref, moved_ref, old_ref, tensor_ref, seen_ref, out_ref, env_ref
):
    gather(moved_ref, old_ref, env_ref)
    total = spread_plain(1, mix_ref, bank_ref, env_ref[...], tensor_ref, out_ref)
    rows, lanes = env_ref.shape[0], out_ref.shape[2]
    odd = jnp.where(pair_ref[...] == now, total, seen_ref[1])
    extra = jnp.concatenate([two_parts(v) for v in (seen_ref[0], odd)], axis=1)
    out_ref[:, rows:, :] = jnp.broadcast_to(extra[None], (out_ref.shape[0], EXTRA, lanes))


def bank_kernel(where_ref, look_ref, *refs):
    tensors, bank_ref = refs[:-1], refs[-1]
    slots, phys, rows, width = bank_ref.shape
    half = width // rows
    for slot, ref in enumerate(tensors):
        for c in range(width // COLS):
            own = [
                jnp.concatenate(
                    [block(ref, h * half + where_ref[0], s, c) for h in range(2)], axis=0
                ).astype(jnp.float32)
                for s in range(phys)
            ]
            for t in range(phys):
                bank_ref[slot, t, :, c * COLS : (c + 1) * COLS] = sum(
                    look_ref[slot, s, t] * own[s] for s in range(phys)
                )


def pick_kernel(pair_ref, *refs):
    kept, outs = refs[:-2], refs[-2:]
    count = len(kept) // 2
    pair = pair_ref[:1, :1]
    for q in range(2):
        value = kept[q * count][...]
        for p in range(1, count):
            value = jnp.where(pair == p, kept[q * count + p][...], value)
        outs[q][...] = value


def second_kernel(moved_ref, tensor_ref, env_ref):
    gather(moved_ref, tensor_ref, env_ref)


def home_kernel(now, pair_ref, moved_ref, tensor_ref, even_ref, odd_ref, six_ref, out_ref, env):
    gather(moved_ref, tensor_ref, env)
    rows = env.shape[0]
    panel = rows // 2
    here = pair_ref[:1, :1] == now
    values = jnp.sum(moved_ref[:, rows:].astype(jnp.float32), axis=0)
    for q, (kept, last) in enumerate(((even_ref, six_ref), (odd_ref, env))):
        result = jnp.where(here, last[...], kept[...])
        value = values[:, q * 128 : (q + 1) * 128]
        extra = two_parts(value[:8] + value[8:])
        extra = jnp.concatenate([extra, jnp.zeros_like(extra)], axis=0)
        width = result.shape[1]
        for h in range(2):
            out_ref[2 * q + h, :, :width] = result[h * panel : (h + 1) * panel]
            out_ref[2 * q + h, :, width:] = extra


def out_kernel(home_ref, out_ref, value_ref):
    fronts, width = out_ref.shape[1], out_ref.shape[3]
    out_ref[0] = home_ref[:, :, :width]
    lane = lax.broadcasted_iota(jnp.int32, (1, 128), 1)
    values = jnp.zeros((1, 128), jnp.float32)
    for f in range(fronts):
        rows = home_ref[f, :, width:].astype(jnp.float32)
        value = jnp.sum(jnp.sum(rows, axis=0, keepdims=True), axis=1, keepdims=True)
        values = jnp.where(lane == f, value, values)
    value_ref[...] = values[:, :fronts]


def mix_kernel(
    width, where_ref, site_ref, kind_ref, operators_ref, probe_ref, mix_ref, look_ref, factor_ref, pair_ref
):
    pair, front = where_ref[1], where_ref[6]
    pair_ref[...] = jnp.zeros_like(pair_ref) + pair
    kind, site = kind_ref[front], site_ref[front]
    phys = probe_ref.shape[0]
    scale = 1.0 / math.sqrt(width)
    for slot in range(2):
        for s in range(phys):
            for t in range(phys):
                row, col = (s, t) if slot == 0 else (t, s)
                own = 1.0 if s == t else 0.0
                factor = jnp.where(site == 2 * pair + slot, operators_ref[kind, row, col], own)
                mix_ref[slot, s, t] = factor
                line = (slot * phys + s) * phys + t
                factor_ref[line : line + 1] = jnp.zeros((1, factor_ref.shape[1]), jnp.float32) + factor
                look_ref[slot, s, t] = probe_ref[row, col] * scale


def cut_kernel(
    where_ref, mine_ref, near_ref, start_ref, other_ref, keep_ref, give_ref, env_ref, sem
):
    core, half, front, parity = where_ref[4], where_ref[5], where_ref[6], where_ref[7]
    panel = other_ref.shape[0]
    copy = pltpu.make_async_copy(
        start_ref.at[front], env_ref.at[pl.ds(pl.multiple_of(half * panel, panel), panel)], sem.at[0]
    )
    copy.start()
    env_ref[pl.ds(pl.multiple_of((1 - half) * panel, panel), panel)] = other_ref[...]
    wide = keep_ref.shape[2]
    mine, near = mine_ref[...], near_ref[...]
    begun = jnp.where(parity == 0, mine, near)
    low, high = begun[..., :wide], begun[..., wide:]
    keep_ref[...] = jnp.where(core == 0, low, high)
    give_ref[...] = jnp.where(core == 0, high, low)
    copy.wait()


SMEM = pl.BlockSpec(memory_space=pltpu.SMEM)
VMEM = pl.BlockSpec(memory_space=pltpu.VMEM)
ANY = pl.BlockSpec(memory_space=pl.ANY)
HBM = pl.BlockSpec(memory_space=pltpu.HBM)


def params():
    return pltpu.CompilerParams(vmem_limit_bytes=16 * MIB)


def shifts(side, by, first):
    pairs = []
    for y in range(side):
        for x in range(side):
            for core in range(2):
                across = (core == 0) == first
                to = y * side + (x + by) % side if across else (y + by) % side * side + x
                pairs.append(((y * side + x) * 2 + core, to * 2 + core))
    return pairs


def in_hbm(arrays):
    return [pltpu.with_memory_space_constraint(a, pltpu.HBM) for a in arrays]


def first_ring(keep, give, core, side):
    bond = ("half", "member")
    other = lax.ppermute(give, bond, twins(side))
    chip = jnp.where(core == 0, jnp.stack([keep, other]), jnp.stack([other, keep]))
    return jnp.stack([chip] + [lax.ppermute(chip, bond, shifts(side, k, True)) for k in range(1, side)])


def second_ring(row, side):
    bond = ("half", "member")
    return [row] + [lax.ppermute(row, bond, shifts(side, m, False)) for m in range(1, side)]


def swap_cores(pieces, side):
    return [lax.ppermute(p, ("half", "member"), twins(side)) for p in pieces]


def twins(side):
    return [(i, i ^ 1) for i in range(2 * side * side)]


def on_device(site_tensors, start_env, operators, op_site, op_kind, probe):
    fronts, panel, width = start_env.shape
    phys = site_tensors.shape[2]
    kinds = operators.shape[0]
    pairs = lax.axis_size("pair")
    pair = lax.axis_index("pair")
    parity = lax.axis_index("parity")
    half = lax.axis_index("half")
    member = lax.axis_index("member")
    members = lax.axis_size("member")
    side = math.isqrt(members)
    rows = 2 * panel
    lanes = 2 * phys * panel
    f32 = jnp.float32
    bf16 = jnp.bfloat16
    core = member % 2
    chip = half * (members // 2) + member // 2
    front = 2 * parity + half
    where = jnp.stack([member, pair, chip // side, chip % side, core, half, front, parity]).astype(jnp.int32)

    mine = jnp.swapaxes(site_tensors[0], 0, 1)
    near = lax.ppermute(mine, "parity", [(0, 1), (1, 0)])
    given = lax.dynamic_index_in_dim(start_env, 2 * parity + 1 - half, 0, keepdims=False)
    other = lax.ppermute(given, "half", [(0, 1), (1, 0)])
    env_shape = jax.ShapeDtypeStruct((rows, width), bf16)
    square = jax.ShapeDtypeStruct((2, phys, phys), f32)
    part = jax.ShapeDtypeStruct((phys, panel, width // 2), bf16)
    bond = ("half", "member")
    mixes, looks, factors, pairs_here = pl.pallas_call(
        functools.partial(mix_kernel, width),
        in_specs=[SMEM] * 5,
        out_specs=[SMEM] * 2 + [VMEM] * 2,
        out_shape=[
            square,
            square,
            jax.ShapeDtypeStruct((2 * phys * phys, COLS), f32),
            jax.ShapeDtypeStruct((8, 128), jnp.int32),
        ],
        compiler_params=params(),
    )(where, op_site, op_kind, operators, probe)
    where, other, mine, near, mixes, looks, factors, pairs_here = lax.optimization_barrier(
        (where, other, mine, near, mixes, looks, factors, pairs_here)
    )
    small = (where, mixes, looks)
    after = lax.all_gather(jnp.where(parity == 0, near, mine), bond, axis=0)
    keep, give, env = pl.pallas_call(
        cut_kernel,
        in_specs=[SMEM] + [VMEM] * 2 + [ANY, VMEM],
        out_specs=[VMEM] * 3,
        out_shape=[part, part, env_shape],
        scratch_shapes=[pltpu.SemaphoreType.DMA((1,))],
        compiler_params=params(),
    )(where, mine, near, start_env, other)
    twin = lax.ppermute(env, bond, twins(side))
    row = first_ring(keep, give, core, side)
    row, twin = lax.optimization_barrier((row, twin))
    pieces = second_ring(row, side)
    swapped = swap_cores(pieces, side)

    def sent_shape(extra):
        return jax.ShapeDtypeStruct((members, rows + extra, lanes), bf16)

    seen_shape = jax.ShapeDtypeStruct((2, 8, 128), f32)

    def exchange(sent):
        return lax.all_to_all(sent, "member", 0, 0, tiled=True)

    sent, seen = pl.pallas_call(
        functools.partial(start_kernel, side),
        in_specs=[SMEM] * 3 + [VMEM] * 2 + [HBM] * side,
        out_specs=[VMEM] * 2,
        out_shape=[jax.ShapeDtypeStruct((members, panel, 2 * lanes), bf16), seen_shape],
        scratch_shapes=[
            pltpu.VMEM((side * side, 2, phys, panel, width // 2), bf16),
            pltpu.SemaphoreType.DMA((width // 2 // COLS, side, side)),
        ],
        compiler_params=params(),
    )(*small, env, twin, *in_hbm(pieces))
    moved = exchange(sent)
    whole = (side * side, 2, 2, phys, panel, width // 2)
    lay_sems = pltpu.SemaphoreType.DMA((2 * side, side))
    everything = pieces + swapped
    env = pl.pallas_call(
        functools.partial(pieces_kernel, side),
        in_specs=[SMEM, VMEM] + [HBM] * (2 * side),
        out_specs=VMEM,
        out_shape=env_shape,
        scratch_shapes=[pltpu.VMEM(whole, bf16), lay_sems],
        compiler_params=params(),
    )(where, moved, *in_hbm(everything))
    evens, odds = [env], []
    twin = lax.ppermute(env, bond, twins(side))
    env, twin, after = lax.optimization_barrier((env, twin, after))
    sent, seen = pl.pallas_call(
        functools.partial(stream_kernel, 0),
        in_specs=[SMEM] * 3 + [VMEM] * 2 + [HBM, VMEM],
        out_specs=[VMEM] * 2,
        out_shape=[jax.ShapeDtypeStruct((members, panel, 2 * lanes), bf16), seen_shape],
        scratch_shapes=[
            pltpu.VMEM(after.shape[:3] + (width // 2,), bf16),
            pltpu.SemaphoreType.DMA((width // 2 // COLS,)),
        ],
        compiler_params=params(),
    )(*small, env, twin, *in_hbm([after]), seen)
    after = pltpu.with_memory_space_constraint(after, pltpu.VMEM)
    before = None
    for now in range(pairs - 1):
        if now > 0:
            sent, seen, env = pl.pallas_call(
                functools.partial(middle_kernel, now),
                in_specs=[VMEM] * 7,
                out_specs=[VMEM] * 3,
                out_shape=[sent_shape(0), seen_shape, env_shape],
                compiler_params=params(),
            )(*vectors, exchange(sent), before, after, seen)
            evens.append(env)
        env = pl.pallas_call(
            second_kernel,
            in_specs=[VMEM] * 2,
            out_specs=VMEM,
            out_shape=env_shape,
            compiler_params=params(),
        )(exchange(sent), after)
        odds.append(env)
        if now == 0:
            env, everything = lax.optimization_barrier((env, everything))
            before = pl.pallas_call(
                functools.partial(lay_kernel, side),
                in_specs=[SMEM] + [HBM] * (2 * side),
                out_specs=ANY,
                out_shape=jax.ShapeDtypeStruct(whole, bf16),
                scratch_shapes=[lay_sems],
                compiler_params=params(),
            )(where, *in_hbm(everything))
            before = pltpu.with_memory_space_constraint(before, pltpu.VMEM)
            bank = pl.pallas_call(
                bank_kernel,
                in_specs=[SMEM] * 2 + [VMEM] * 2,
                out_specs=VMEM,
                out_shape=jax.ShapeDtypeStruct((2, phys, rows, width), f32),
                compiler_params=params(),
            )(where, looks, before, after)
            vectors = (pairs_here, factors, bank)
        if now == pairs - 2:
            env, *kept = lax.optimization_barrier((env, *evens, *odds))
            picked = pl.pallas_call(
                pick_kernel,
                in_specs=[VMEM] * (1 + len(kept)),
                out_specs=[VMEM] * 2,
                out_shape=[env_shape] * 2,
                compiler_params=params(),
            )(pairs_here, *kept)
        env = lax.ppermute(env, "pair", [(now, now + 1)])
        if now == pairs - 2:
            env, picked = lax.optimization_barrier((env, picked))
        sent, seen = pl.pallas_call(
            functools.partial(first_kernel, now + 1),
            in_specs=[VMEM] * 6,
            out_specs=[VMEM] * 2,
            out_shape=[sent_shape(0), seen_shape],
            compiler_params=params(),
        )(*vectors, env, before, seen)
    moved = exchange(sent)
    sent, env = pl.pallas_call(
        functools.partial(end_kernel, pairs - 1),
        in_specs=[VMEM] * 7,
        out_specs=[VMEM] * 2,
        out_shape=[sent_shape(EXTRA), env_shape],
        compiler_params=params(),
    )(*vectors, moved, before, after, seen)
    homeward = pl.pallas_call(
        functools.partial(home_kernel, pairs - 1),
        in_specs=[VMEM] * 6,
        out_specs=VMEM,
        out_shape=jax.ShapeDtypeStruct((fronts, panel, width + 128), bf16),
        scratch_shapes=[pltpu.VMEM((rows, width), bf16)],
        compiler_params=params(),
    )(pairs_here, exchange(sent), after, *picked, env)
    home = lax.all_to_all(homeward, ("parity", "half"), 0, 0, tiled=True)
    out, values = pl.pallas_call(
        out_kernel,
        in_specs=[VMEM],
        out_specs=[VMEM] * 2,
        out_shape=[
            jax.ShapeDtypeStruct((1, fronts, panel, width), bf16),
            jax.ShapeDtypeStruct((1, fronts), f32),
        ],
        compiler_params=params(),
    )(home)
    return out, values.reshape(fronts, 1)


def solution(mesh):
    links, peers = mesh.devices.shape
    devices = mesh.devices.reshape(links // 2, 2, 2, peers // 2)
    chain, bond = ("pair", "parity"), ("half", "member")
    placed = (P(chain, bond, None, None), P(None, bond, None), P(), P(), P(), P())
    return jax.shard_map(
        on_device,
        mesh=Mesh(devices, chain + bond),
        in_specs=placed,
        out_specs=(P(chain, None, bond, None), P(None, chain)),
        check_vma=False,
    )
```

```python
import functools
import math

import jax
import jax.numpy as jnp
from jax import lax
from jax.experimental import pallas as pl
from jax.experimental.pallas import tpu as pltpu
from jax.sharding import Mesh
from jax.sharding import PartitionSpec as P

EXTRA = 16
MIB = 1 << 20
COLS = 256


def two_parts(value):
    high = value.astype(jnp.bfloat16).astype(jnp.float32)
    return jnp.concatenate([high, value - high], axis=0).astype(jnp.bfloat16)


def for_first_pair(kernel):
    def guarded(static, where_ref, *refs):
        pl.when(where_ref[1] == 0)(functools.partial(kernel, static, where_ref, *refs))

    return guarded


def columns(tensor_ref, t, c):
    if len(tensor_ref.shape) == 4:
        return tensor_ref[:, t, :, c * COLS : (c + 1) * COLS].reshape(-1, COLS)
    per = tensor_ref.shape[5] // COLS
    at = c % per * COLS
    return tensor_ref[:, c // per, :, t, :, at : at + COLS].reshape(-1, COLS)


def block(tensor_ref, d, s, c):
    if len(tensor_ref.shape) == 4:
        return tensor_ref[d, s, :, c * COLS : (c + 1) * COLS].reshape(-1, COLS)
    per = tensor_ref.shape[5] // COLS
    at = c % per * COLS
    return tensor_ref[d // 2, c // per, d % 2, s, :, at : at + COLS].reshape(-1, COLS)


def spread(slot, where_ref, mix_ref, look_ref, env, tensor_ref, out_ref, arrived=None):
    width = env.shape[1]
    phys = mix_ref.shape[1]
    panel = env.shape[0] // 2
    half = width // panel // 2
    mem = where_ref[0]
    total = jnp.zeros((1, 128), jnp.float32)
    for c in range(width // COLS):
        if arrived is not None:
            arrived[c]()
        prods = [
            jnp.dot(env, columns(tensor_ref, t, c), preferred_element_type=jnp.float32)
            for t in range(phys)
        ]
        for s in range(phys):
            own = jnp.concatenate(
                [block(tensor_ref, h * half + mem, s, c) for h in range(2)], axis=0
            ).astype(jnp.float32)
            seen = own * sum(look_ref[slot, s, t] * prods[t] for t in range(phys))
            line = jnp.sum(seen, axis=0, keepdims=True)
            total += sum(line[:, b : b + 128] for b in range(0, COLS, 128))
        mixed = [sum(mix_ref[slot, s, t] * prods[t] for t in range(phys)) for s in range(phys)]
        tall = jnp.concatenate(
            [mixed[s][h * panel : (h + 1) * panel] for h in range(2) for s in range(phys)], axis=0
        )
        turned = tall.astype(jnp.bfloat16).T.reshape(COLS // panel, panel, 2 * phys * panel)
        first = c * (COLS // panel)
        h, first = first // half, first % half
        out_ref[first : first + COLS // panel, h * panel : (h + 1) * panel, :] = turned
    return total


def gather(moved_ref, tensor_ref, env_ref):
    rows, width = env_ref.shape
    half = moved_ref.shape[0]
    if moved_ref.shape[2] < COLS:
        left = [
            jnp.concatenate([moved_ref[g, :rows], moved_ref[g, rows : 2 * rows]], axis=1)
            for g in range(half)
        ]
    elif moved_ref.shape[1] < rows:
        left = [
            jnp.concatenate([moved_ref[g], moved_ref[g + 1]], axis=0) for g in range(0, half, 2)
        ]
    else:
        left = [moved_ref[g, :rows] for g in range(half)]
    left = jnp.concatenate(left, axis=1)
    for c in range(width // COLS):
        right = jnp.concatenate(
            [
                block(tensor_ref, h * half + g, slice(None), c)
                for g in range(half)
                for h in range(2)
            ],
            axis=0,
        )
        env_ref[:, c * COLS : (c + 1) * COLS] = jnp.dot(
            left, right, preferred_element_type=jnp.float32
        ).astype(jnp.bfloat16)


def chip_of(side, where_ref, at, m, k):
    y, x = where_ref[2], where_ref[3]
    along = lax.rem(y + side - jnp.where(at == 0, m, k), side)
    across = lax.rem(x + side - jnp.where(at == 0, k, m), side)
    return along * side + across


def lay(side, where_ref, pieces, tensor_ref, sems):
    copies = []
    for i, ref in enumerate(pieces):
        at = where_ref[4] if i < side else 1 - where_ref[4]
        for k in range(side):
            place = tensor_ref.at[chip_of(side, where_ref, at, i % side, k), at]
            copies.append(pltpu.make_async_copy(ref.at[k], place, sems.at[i, k]))
    for copy in copies:
        copy.start()
    return copies


def lay_kernel(side, where_ref, *refs):
    for copy in lay(side, where_ref, refs[:-2], refs[-2], refs[-1]):
        copy.wait()


@for_first_pair
def pieces_kernel(side, where_ref, moved_ref, *refs):
    pieces, (env_ref, tensor, sems) = refs[:-3], refs[-3:]
    copies = lay(side, where_ref, pieces, tensor, sems)
    chips, wide = tensor.shape[0], tensor.shape[5]
    left = jnp.concatenate(
        [
            jnp.concatenate([moved_ref[g], moved_ref[g + 1]], axis=0) for g in range(0, chips, 2)
        ],
        axis=1,
    )
    for part in range(2):
        at = where_ref[4] if part == 0 else 1 - where_ref[4]
        for copy in copies[part * side * side : (part + 1) * side * side]:
            copy.wait()
        for c in range(wide // COLS):
            cols = slice(c * COLS, (c + 1) * COLS)
            right = jnp.concatenate(
                [
                    tensor[(h * chips + g) // 2, at, g % 2, :, :, cols].reshape(-1, COLS)
                    for g in range(chips)
                    for h in range(2)
                ],
                axis=0,
            )
            place = pl.ds(pl.multiple_of(at * wide + c * COLS, COLS), COLS)
            env_ref[:, place] = jnp.dot(
                left, right, preferred_element_type=jnp.float32
            ).astype(jnp.bfloat16)


@for_first_pair
def stream_kernel(
    now, where_ref, mix_ref, look_ref, env_ref, twin_ref, tensor_ref, seen_ref, out_ref, new_ref, held, sems
):
    core = where_ref[4]
    peers, phys, panel, wide = held.shape
    copies = []
    for c in range(wide // COLS):
        place = pl.ds(pl.multiple_of(core * wide + c * COLS, COLS), COLS)
        copies.append(
            pltpu.make_async_copy(
                tensor_ref.at[:, :, :, place], held.at[:, :, :, pl.ds(c * COLS, COLS)], sems.at[c]
            )
        )
        copies[-1].start()
    own, twin = env_ref[...], twin_ref[...]
    env = jnp.concatenate(
        [jnp.where(core == 0, own, twin), jnp.where(core == 0, twin, own)], axis=0
    )
    even = where_ref[0] - core
    total = jnp.zeros(new_ref.shape[1:], jnp.float32)
    for c, copy in enumerate(copies):
        copy.wait()
        cols = slice(c * COLS, (c + 1) * COLS)
        prods = [
            jnp.dot(env, held[:, t, :, cols].reshape(-1, COLS), preferred_element_type=jnp.float32)
            for t in range(phys)
        ]
        for s in range(phys):
            rows = [held[h * (peers // 2) + even + o, s, :, cols] for o in range(2) for h in range(2)]
            seen = jnp.concatenate(rows, axis=0).astype(jnp.float32)
            seen = seen * sum(look_ref[1, s, t] * prods[t] for t in range(phys))
            seen = jnp.sum(seen.reshape(-1, 8, COLS), axis=0)
            total += sum(seen[:, b : b + 128] for b in range(0, COLS, 128))
        mixed = [sum(mix_ref[1, s, t] * prods[t] for t in range(phys)) for s in range(phys)]
        tall = [mixed[s][q * panel : (q + 1) * panel] for q in range(4) for s in range(phys)]
        turned = jnp.concatenate(tall, axis=0).astype(jnp.bfloat16).T
        per = COLS // panel
        out_ref[c * per : (c + 1) * per] = turned.reshape(per, panel, 4 * phys * panel)
    new_ref[0] = seen_ref[0]
    new_ref[1] = total


def load(side, where_ref, pieces, tensor_ref, sems):
    blocks = []
    for c in range(tensor_ref.shape[4] // COLS):
        cols = pl.ds(c * COLS, COLS)
        copies = []
        for m, ref in enumerate(pieces):
            for k in range(side):
                chip = chip_of(side, where_ref, where_ref[4], m, k)
                copies.append(
                    pltpu.make_async_copy(
                        ref.at[k, :, :, :, cols], tensor_ref.at[chip, :, :, :, cols], sems.at[c, m, k]
                    )
                )
        for copy in copies:
            copy.start()
        blocks.append(copies)
    return blocks


@for_first_pair
def start_kernel(side, where_ref, mix_ref, look_ref, env_ref, twin_ref, *refs):
    pieces, (out_ref, new_ref, tensor, sems) = refs[:-4], refs[-4:]
    core = where_ref[4]
    blocks = load(side, where_ref, pieces, tensor, sems)
    own, twin = env_ref[...], twin_ref[...]
    env = jnp.concatenate(
        [jnp.where(core == 0, own, twin), jnp.where(core == 0, twin, own)], axis=0
    )
    chips, _, phys, panel, wide = tensor.shape
    mem = where_ref[0] // 2
    total = jnp.zeros((1, 128), jnp.float32)
    for c, copies in enumerate(blocks):
        for copy in copies:
            copy.wait()
        cols = slice(c * COLS, (c + 1) * COLS)
        prods = [
            jnp.dot(
                env, tensor[:, :, t, :, cols].reshape(-1, COLS), preferred_element_type=jnp.float32
            )
            for t in range(phys)
        ]
        for s in range(phys):
            rows = [tensor[h * (chips // 2) + mem, o, s, :, cols] for o in range(2) for h in range(2)]
            seen = jnp.concatenate(rows, axis=0).astype(jnp.float32)
            seen = seen * sum(look_ref[0, s, t] * prods[t] for t in range(phys))
            line = jnp.sum(seen, axis=0, keepdims=True)
            total += sum(line[:, b : b + 128] for b in range(0, COLS, 128))
        mixed = [sum(mix_ref[0, s, t] * prods[t] for t in range(phys)) for s in range(phys)]
        tall = [mixed[s][q * panel : (q + 1) * panel] for q in range(4) for s in range(phys)]
        turned = jnp.concatenate(tall, axis=0).astype(jnp.bfloat16).T
        per = COLS // panel
        out_ref[c * per : (c + 1) * per] = turned.reshape(per, panel, 4 * phys * panel)
    first_row = lax.broadcasted_iota(jnp.int32, new_ref.shape[1:], 0) == 0
    total = jnp.where(first_row, jnp.broadcast_to(total, new_ref.shape[1:]), 0.0)
    new_ref[...] = jnp.broadcast_to(total[None], new_ref.shape)


def spread_plain(slot, mix_ref, bank_ref, env, tensor_ref, out_ref):
    width = env.shape[1]
    phys = bank_ref.shape[1]
    panel = env.shape[0] // 2
    half = width // panel // 2
    total = jnp.zeros((8, 128), jnp.float32)
    for c in range(width // COLS):
        prods = [
            jnp.dot(env, columns(tensor_ref, t, c), preferred_element_type=jnp.float32)
            for t in range(phys)
        ]
        seen = sum(bank_ref[slot, t, :, c * COLS : (c + 1) * COLS] * prods[t] for t in range(phys))
        seen = jnp.sum(seen.reshape(-1, 8, COLS), axis=0)
        total += sum(seen[:, b : b + 128] for b in range(0, COLS, 128))

        def factor(s, t):
            row = slot * phys * phys + s * phys + t
            return mix_ref[row : row + 1]

        mixed = [sum(factor(s, t) * prods[t] for t in range(phys)) for s in range(phys)]
        tall = jnp.concatenate(
            [mixed[s][h * panel : (h + 1) * panel] for h in range(2) for s in range(phys)], axis=0
        )
        turned = tall.astype(jnp.bfloat16).T.reshape(COLS // panel, panel, 2 * phys * panel)
        first = c * (COLS // panel)
        h, first = first // half, first % half
        lanes = out_ref.shape[2]
        for part in range(turned.shape[2] // lanes):
            top = part * 2 * panel + h * panel
            out_ref[first : first + COLS // panel, top : top + panel, :] = turned[
                :, :, part * lanes : (part + 1) * lanes
            ]
    return total


def first_kernel(now, pair_ref, mix_ref, bank_ref, env_ref, tensor_ref, seen_ref, out_ref, new_ref):
    total = spread_plain(0, mix_ref, bank_ref, env_ref[...], tensor_ref, out_ref)
    new_ref[0] = jnp.where(pair_ref[...] == now, total, seen_ref[0])
    new_ref[1] = seen_ref[1]


def middle_kernel(
    now, pair_ref, mix_ref, bank_ref, moved_ref, old_ref, tensor_ref, seen_ref, out_ref, new_ref, env_ref
):
    gather(moved_ref, old_ref, env_ref)
    total = spread_plain(1, mix_ref, bank_ref, env_ref[...], tensor_ref, out_ref)
    new_ref[0] = seen_ref[0]
    new_ref[1] = jnp.where(pair_ref[...] == now, total, seen_ref[1])


def end_kernel(
    now, pair_ref, mix_ref, bank_ref, moved_ref, old_ref, tensor_ref, seen_ref, out_ref, env_ref
):
    gather(moved_ref, old_ref, env_ref)
    total = spread_plain(1, mix_ref, bank_ref, env_ref[...], tensor_ref, out_ref)
    rows, lanes = 2 * env_ref.shape[0], out_ref.shape[2]
    odd = jnp.where(pair_ref[...] == now, total, seen_ref[1])
    extra = [two_parts(v[:4] + v[4:]).astype(jnp.float32) for v in (seen_ref[0], odd)]
    extra = jnp.concatenate(extra, axis=0).astype(jnp.bfloat16)
    out_ref[:, rows:, :] = jnp.broadcast_to(extra[None], (out_ref.shape[0], EXTRA, lanes))


def bank_kernel(where_ref, look_ref, *refs):
    tensors, bank_ref = refs[:-1], refs[-1]
    slots, phys, rows, width = bank_ref.shape
    half = width // rows
    for slot, ref in enumerate(tensors):
        for c in range(width // COLS):
            own = [
                jnp.concatenate(
                    [block(ref, h * half + where_ref[0], s, c) for h in range(2)], axis=0
                ).astype(jnp.float32)
                for s in range(phys)
            ]
            for t in range(phys):
                bank_ref[slot, t, :, c * COLS : (c + 1) * COLS] = sum(
                    look_ref[slot, s, t] * own[s] for s in range(phys)
                )


def pick_kernel(pair_ref, *refs):
    kept, outs = refs[:-2], refs[-2:]
    count = len(kept) // 2
    pair = pair_ref[:1, :1]
    for q in range(2):
        value = kept[q * count][...]
        for p in range(1, count):
            value = jnp.where(pair == p, kept[q * count + p][...], value)
        outs[q][...] = value


def second_kernel(moved_ref, tensor_ref, env_ref):
    gather(moved_ref, tensor_ref, env_ref)


def home_kernel(now, pair_ref, moved_ref, tensor_ref, even_ref, odd_ref, six_ref, out_ref, env):
    gather(moved_ref, tensor_ref, env)
    rows = env.shape[0]
    panel = rows // 2
    here = pair_ref[:1, :1] == now
    values = jnp.sum(moved_ref[:, 2 * rows :].astype(jnp.float32), axis=0)
    for q, (kept, last) in enumerate(((even_ref, six_ref), (odd_ref, env))):
        result = jnp.where(here, last[...], kept[...])
        value = values[q * 8 : q * 8 + 4] + values[q * 8 + 4 : q * 8 + 8]
        extra = two_parts(jnp.concatenate([value, jnp.zeros_like(value)], axis=0))
        extra = jnp.concatenate([extra, jnp.zeros_like(extra)], axis=0)
        width = result.shape[1]
        for h in range(2):
            out_ref[2 * q + h, :, :width] = result[h * panel : (h + 1) * panel]
            out_ref[2 * q + h, :, width:] = extra


def out_kernel(home_ref, out_ref, value_ref):
    fronts, width = out_ref.shape[1], out_ref.shape[3]
    out_ref[0] = home_ref[:, :, :width]
    lane = lax.broadcasted_iota(jnp.int32, (1, 128), 1)
    values = jnp.zeros((1, 128), jnp.float32)
    for f in range(fronts):
        rows = home_ref[f, :, width:].astype(jnp.float32)
        value = jnp.sum(jnp.sum(rows, axis=0, keepdims=True), axis=1, keepdims=True)
        values = jnp.where(lane == f, value, values)
    value_ref[...] = values[:, :fronts]


def mix_kernel(
    width, where_ref, site_ref, kind_ref, operators_ref, probe_ref, mix_ref, look_ref, factor_ref, pair_ref
):
    pair, front = where_ref[1], where_ref[6]
    pair_ref[...] = jnp.zeros_like(pair_ref) + pair
    kind, site = kind_ref[front], site_ref[front]
    phys = probe_ref.shape[0]
    scale = 1.0 / math.sqrt(width)
    for slot in range(2):
        for s in range(phys):
            for t in range(phys):
                row, col = (s, t) if slot == 0 else (t, s)
                own = 1.0 if s == t else 0.0
                factor = jnp.where(site == 2 * pair + slot, operators_ref[kind, row, col], own)
                mix_ref[slot, s, t] = factor
                line = (slot * phys + s) * phys + t
                factor_ref[line : line + 1] = jnp.zeros((1, factor_ref.shape[1]), jnp.float32) + factor
                look_ref[slot, s, t] = probe_ref[row, col] * scale


def cut_kernel(
    where_ref, mine_ref, near_ref, start_ref, other_ref, keep_ref, give_ref, env_ref, sem
):
    core, half, front, parity = where_ref[4], where_ref[5], where_ref[6], where_ref[7]
    panel = other_ref.shape[0]
    copy = pltpu.make_async_copy(
        start_ref.at[front], env_ref.at[pl.ds(pl.multiple_of(half * panel, panel), panel)], sem.at[0]
    )
    copy.start()
    env_ref[pl.ds(pl.multiple_of((1 - half) * panel, panel), panel)] = other_ref[...]
    wide = keep_ref.shape[2]
    mine, near = mine_ref[...], near_ref[...]
    begun = jnp.where(parity == 0, mine, near)
    low, high = begun[..., :wide], begun[..., wide:]
    keep_ref[...] = jnp.where(core == 0, low, high)
    give_ref[...] = jnp.where(core == 0, high, low)
    copy.wait()


SMEM = pl.BlockSpec(memory_space=pltpu.SMEM)
VMEM = pl.BlockSpec(memory_space=pltpu.VMEM)
ANY = pl.BlockSpec(memory_space=pl.ANY)
HBM = pl.BlockSpec(memory_space=pltpu.HBM)


def params():
    return pltpu.CompilerParams(vmem_limit_bytes=16 * MIB)


def shifts(side, by, first):
    pairs = []
    for y in range(side):
        for x in range(side):
            for core in range(2):
                across = (core == 0) == first
                to = y * side + (x + by) % side if across else (y + by) % side * side + x
                pairs.append(((y * side + x) * 2 + core, to * 2 + core))
    return pairs


def in_hbm(arrays):
    return [pltpu.with_memory_space_constraint(a, pltpu.HBM) for a in arrays]


def first_ring(keep, give, core, side):
    bond = ("half", "member")
    other = lax.ppermute(give, bond, twins(side))
    chip = jnp.where(core == 0, jnp.stack([keep, other]), jnp.stack([other, keep]))
    return jnp.stack([chip] + [lax.ppermute(chip, bond, shifts(side, k, True)) for k in range(1, side)])


def second_ring(row, side):
    bond = ("half", "member")
    return [row] + [lax.ppermute(row, bond, shifts(side, m, False)) for m in range(1, side)]


def swap_cores(pieces, side):
    return [lax.ppermute(p, ("half", "member"), twins(side)) for p in pieces]


def twins(side):
    return [(i, i ^ 1) for i in range(2 * side * side)]


def on_device(site_tensors, start_env, operators, op_site, op_kind, probe):
    fronts, panel, width = start_env.shape
    phys = site_tensors.shape[2]
    kinds = operators.shape[0]
    pairs = lax.axis_size("pair")
    pair = lax.axis_index("pair")
    parity = lax.axis_index("parity")
    half = lax.axis_index("half")
    member = lax.axis_index("member")
    members = lax.axis_size("member")
    side = math.isqrt(members)
    rows = 2 * panel
    lanes = 2 * phys * panel
    f32 = jnp.float32
    bf16 = jnp.bfloat16
    core = member % 2
    chip = half * (members // 2) + member // 2
    front = 2 * parity + half
    where = jnp.stack([member, pair, chip // side, chip % side, core, half, front, parity]).astype(jnp.int32)

    mine = jnp.swapaxes(site_tensors[0], 0, 1)
    near = lax.ppermute(mine, "parity", [(0, 1), (1, 0)])
    given = lax.dynamic_index_in_dim(start_env, 2 * parity + 1 - half, 0, keepdims=False)
    other = lax.ppermute(given, "half", [(0, 1), (1, 0)])
    env_shape = jax.ShapeDtypeStruct((rows, width), bf16)
    square = jax.ShapeDtypeStruct((2, phys, phys), f32)
    part = jax.ShapeDtypeStruct((phys, panel, width // 2), bf16)
    bond = ("half", "member")
    mixes, looks, factors, pairs_here = pl.pallas_call(
        functools.partial(mix_kernel, width),
        in_specs=[SMEM] * 5,
        out_specs=[SMEM] * 2 + [VMEM] * 2,
        out_shape=[
            square,
            square,
            jax.ShapeDtypeStruct((2 * phys * phys, COLS), f32),
            jax.ShapeDtypeStruct((8, 128), jnp.int32),
        ],
        compiler_params=params(),
    )(where, op_site, op_kind, operators, probe)
    where, other, mine, near, mixes, looks, factors, pairs_here = lax.optimization_barrier(
        (where, other, mine, near, mixes, looks, factors, pairs_here)
    )
    small = (where, mixes, looks)
    after = lax.all_gather(jnp.where(parity == 0, near, mine), bond, axis=0)
    keep, give, env = pl.pallas_call(
        cut_kernel,
        in_specs=[SMEM] + [VMEM] * 2 + [ANY, VMEM],
        out_specs=[VMEM] * 3,
        out_shape=[part, part, env_shape],
        scratch_shapes=[pltpu.SemaphoreType.DMA((1,))],
        compiler_params=params(),
    )(where, mine, near, start_env, other)
    twin = lax.ppermute(env, bond, twins(side))
    row = first_ring(keep, give, core, side)
    row, twin = lax.optimization_barrier((row, twin))
    pieces = second_ring(row, side)
    swapped = swap_cores(pieces, side)

    def sent_shape(extra):
        return jax.ShapeDtypeStruct((members, rows + extra, lanes), bf16)

    seen_shape = jax.ShapeDtypeStruct((2, 8, 128), f32)

    def exchange(sent):
        return lax.all_to_all(sent, "member", 0, 0, tiled=True)

    sent, seen = pl.pallas_call(
        functools.partial(start_kernel, side),
        in_specs=[SMEM] * 3 + [VMEM] * 2 + [HBM] * side,
        out_specs=[VMEM] * 2,
        out_shape=[jax.ShapeDtypeStruct((members, panel, 2 * lanes), bf16), seen_shape],
        scratch_shapes=[
            pltpu.VMEM((side * side, 2, phys, panel, width // 2), bf16),
            pltpu.SemaphoreType.DMA((width // 2 // COLS, side, side)),
        ],
        compiler_params=params(),
    )(*small, env, twin, *in_hbm(pieces))
    moved = exchange(sent)
    whole = (side * side, 2, 2, phys, panel, width // 2)
    lay_sems = pltpu.SemaphoreType.DMA((2 * side, side))
    everything = pieces + swapped
    env = pl.pallas_call(
        functools.partial(pieces_kernel, side),
        in_specs=[SMEM, VMEM] + [HBM] * (2 * side),
        out_specs=VMEM,
        out_shape=env_shape,
        scratch_shapes=[pltpu.VMEM(whole, bf16), lay_sems],
        compiler_params=params(),
    )(where, moved, *in_hbm(everything))
    evens, odds = [env], []
    twin = lax.ppermute(env, bond, twins(side))
    env, twin, after = lax.optimization_barrier((env, twin, after))
    sent, seen = pl.pallas_call(
        functools.partial(stream_kernel, 0),
        in_specs=[SMEM] * 3 + [VMEM] * 2 + [HBM, VMEM],
        out_specs=[VMEM] * 2,
        out_shape=[jax.ShapeDtypeStruct((members, panel, 2 * lanes), bf16), seen_shape],
        scratch_shapes=[
            pltpu.VMEM(after.shape[:3] + (width // 2,), bf16),
            pltpu.SemaphoreType.DMA((width // 2 // COLS,)),
        ],
        compiler_params=params(),
    )(*small, env, twin, *in_hbm([after]), seen)
    after = pltpu.with_memory_space_constraint(after, pltpu.VMEM)
    before = None
    for now in range(pairs - 1):
        if now > 0:
            sent, seen, env = pl.pallas_call(
                functools.partial(middle_kernel, now),
                in_specs=[VMEM] * 7,
                out_specs=[VMEM] * 3,
                out_shape=[sent_shape(0), seen_shape, env_shape],
                compiler_params=params(),
            )(*vectors, exchange(sent), before, after, seen)
            evens.append(env)
        env = pl.pallas_call(
            second_kernel,
            in_specs=[VMEM] * 2,
            out_specs=VMEM,
            out_shape=env_shape,
            compiler_params=params(),
        )(exchange(sent), after)
        odds.append(env)
        if now == 0:
            env, everything = lax.optimization_barrier((env, everything))
            before = pl.pallas_call(
                functools.partial(lay_kernel, side),
                in_specs=[SMEM] + [HBM] * (2 * side),
                out_specs=ANY,
                out_shape=jax.ShapeDtypeStruct(whole, bf16),
                scratch_shapes=[lay_sems],
                compiler_params=params(),
            )(where, *in_hbm(everything))
            before = pltpu.with_memory_space_constraint(before, pltpu.VMEM)
            bank = pl.pallas_call(
                bank_kernel,
                in_specs=[SMEM] * 2 + [VMEM] * 2,
                out_specs=VMEM,
                out_shape=jax.ShapeDtypeStruct((2, phys, rows, width), f32),
                compiler_params=params(),
            )(where, looks, before, after)
            vectors = (pairs_here, factors, bank)
        if now == pairs - 2:
            env, *kept = lax.optimization_barrier((env, *evens, *odds))
            picked = pl.pallas_call(
                pick_kernel,
                in_specs=[VMEM] * (1 + len(kept)),
                out_specs=[VMEM] * 2,
                out_shape=[env_shape] * 2,
                compiler_params=params(),
            )(pairs_here, *kept)
        env = lax.ppermute(env, "pair", [(now, now + 1)])
        if now == pairs - 2:
            env, picked = lax.optimization_barrier((env, picked))
        sent, seen = pl.pallas_call(
            functools.partial(first_kernel, now + 1),
            in_specs=[VMEM] * 6,
            out_specs=[VMEM] * 2,
            out_shape=[sent_shape(0), seen_shape],
            compiler_params=params(),
        )(*vectors, env, before, seen)
    moved = exchange(sent)
    sent, env = pl.pallas_call(
        functools.partial(end_kernel, pairs - 1),
        in_specs=[VMEM] * 7,
        out_specs=[VMEM] * 2,
        out_shape=[jax.ShapeDtypeStruct((members, 2 * rows + EXTRA, lanes // 2), bf16), env_shape],
        compiler_params=params(),
    )(*vectors, moved, before, after, seen)
    homeward = pl.pallas_call(
        functools.partial(home_kernel, pairs - 1),
        in_specs=[VMEM] * 6,
        out_specs=VMEM,
        out_shape=jax.ShapeDtypeStruct((fronts, panel, width + 128), bf16),
        scratch_shapes=[pltpu.VMEM((rows, width), bf16)],
        compiler_params=params(),
    )(pairs_here, exchange(sent), after, *picked, env)
    home = lax.all_to_all(homeward, ("parity", "half"), 0, 0, tiled=True)
    out, values = pl.pallas_call(
        out_kernel,
        in_specs=[VMEM],
        out_specs=[VMEM] * 2,
        out_shape=[
            jax.ShapeDtypeStruct((1, fronts, panel, width), bf16),
            jax.ShapeDtypeStruct((1, fronts), f32),
        ],
        compiler_params=params(),
    )(home)
    return out, values.reshape(fronts, 1)


def solution(mesh):
    links, peers = mesh.devices.shape
    devices = mesh.devices.reshape(links // 2, 2, 2, peers // 2)
    chain, bond = ("pair", "parity"), ("half", "member")
    placed = (P(chain, bond, None, None), P(None, bond, None), P(), P(), P(), P())
    return jax.shard_map(
        on_device,
        mesh=Mesh(devices, chain + bond),
        in_specs=placed,
        out_specs=(P(chain, None, bond, None), P(None, chain)),
        check_vma=False,
    )
```
